32 devices in a mesh: groups: 2 (over y), nodes: 4 (over z), cols: 4 (over x, core).
Axes of the slice: x: 2, y: 2, z: 4, core: 2. Of those that a mesh axis runs over, the one named last changes fastest.
Arguments:
- forces: float32 [256, 16384], P('cols', ('groups', 'nodes')), parts along dimension 1, may hold values from -150 to 150
- couplings: float32 [3, 16384], P(None, ('groups', 'nodes')), parts along dimension 1, may hold values from 0.1 to 1
- ground: float32 [16384], P(('groups', 'nodes')), parts along dimension 0, may hold values from 0.3 to 3
- precond: float32 [128, 128, 128], P(('groups', 'nodes')), parts along dimension 0, may hold values from -3 to 3, as said below
Outputs:
- modes: float32 [256, 16384], P('cols', ('groups', 'nodes')), parts along dimension 1
- tile: float32 [512, 256], P(('groups', 'cols'), 'nodes'), parts along dimension 0
The draws below stay inside these ranges and needn't reach their ends.
There are 2 independent parts, one for each index of `groups`. The reference program is written for one: setup_inputs(seed, part) draws one part's arguments, and reference() takes and returns one part's arrays. A program takes and returns all parts, laid end to end along the dimension named above; each array names one. Nothing has to cross between parts.
Inputs may be any that keep to these rules, and one draw needn't show every extreme that they name: `precond`: each matrix is symmetric positive definite.
All inputs are finite; a program needn't handle non-finite values.
Results may differ from the reference program's by a relative error of at most 0.0003.
Values sent between devices are 32-bit elements; how exact they have to be, the bound alone decides.
No kernel may reach another device: no remote copies, remote signals or barrier semaphores. Data moves between devices by JAX's collectives and lax.ppermute only.
A program may use at most 64 MiB of HBM per device.

```python
import math
import jax
import jax.numpy as jnp
from jax import lax

COLS = 256
BLK = 128
GRID_X = 32
GRID_Y = 32
ITERS = 2
NDOF = 8192


def draw_forces(key, part):
    key = jax.random.fold_in(key, 11)
    keys = jax.random.split(key, 3)
    place = (jnp.arange(NDOF, dtype=jnp.float32) + 0.5) / NDOF
    rising = jnp.exp(jnp.log(3.0) * place)
    weight = jax.random.uniform(keys[2], (COLS, 1), jnp.float32, 0.5, 1.5)
    base = jnp.clip(jax.random.normal(keys[0], (COLS, NDOF), jnp.float32), -6.0, 6.0)
    common = jnp.clip(jax.random.normal(keys[1], (NDOF,), jnp.float32), -6.0, 6.0)
    return (base + weight * common[None, :]) * rising[None, :]


def draw_precond(key, part):
    key = jax.random.fold_in(key, 23)
    keys = jax.random.split(key, 2)
    count = NDOF // BLK
    raw = jax.random.uniform(keys[0], (count, BLK, BLK), jnp.float32, -0.03, 0.03)
    sym = raw + jnp.swapaxes(raw, 1, 2)
    scale = jnp.exp(jax.random.uniform(keys[1], (count, BLK), jnp.float32, jnp.log(0.5), jnp.log(2.0)))
    root = jnp.sqrt(scale)
    return root[:, :, None] * root[:, None, :] * (jnp.eye(BLK, dtype=jnp.float32)[None] + sym)


def block_levels(own_key, extent, pieces, low, largest):
    def one(dim, parts):
        heights = jax.random.uniform(jax.random.fold_in(jax.random.fold_in(own_key, 6), dim), (parts,), jnp.float32, low / len(pieces), largest / len(pieces))
        return jnp.repeat(jnp.exp(heights), extent[dim] // parts).reshape((-1,) + (1,) * (len(extent) - dim - 1))

    level = one(*pieces[0])
    for cut in pieces[1:]:
        level = level * one(*cut)
    return level


def setup_inputs(seed: int = 0, part: int = 0) -> dict:
    seeds = jax.random.split(jax.random.key(seed), 5)
    own_keys = jax.random.split(jax.random.fold_in(seeds[4], part), 5)
    return {
        "forces": draw_forces(jax.random.fold_in(jax.random.fold_in(seeds[4], part), 71), part),
        "couplings": jnp.clip(jnp.exp(math.log(1.0) - 2.3025851 * jax.random.uniform(own_keys[1], (3, NDOF), jnp.float32) ** block_levels(own_keys[1], (3, NDOF), ((1, 4),), -0.2, 0.2)), 0.1, 1.0),
        "ground": jnp.clip(jnp.exp(math.log(3.0) - 2.3025851 * jax.random.uniform(own_keys[2], (NDOF,), jnp.float32) ** block_levels(own_keys[2], (NDOF,), ((0, 4),), -0.2, 0.2)), 0.3, 3.0),
        "precond": draw_precond(jax.random.fold_in(jax.random.fold_in(seeds[4], part), 71), part),
    }


def behind(values, step):
    pad = jnp.zeros(values.shape[:-1] + (step,), values.dtype)
    return jnp.concatenate([pad, values[..., :-step]], axis=-1)


def ahead(values, step):
    pad = jnp.zeros(values.shape[:-1] + (step,), values.dtype)
    return jnp.concatenate([values[..., step:], pad], axis=-1)


def spring_rows(couplings):
    index = jnp.arange(NDOF, dtype=jnp.int32)
    mask_x = ((index % GRID_X) < GRID_X - 1).astype(jnp.float32)
    mask_y = (((index // GRID_X) % GRID_Y) < GRID_Y - 1).astype(jnp.float32)
    return [couplings[0] * mask_x, couplings[1] * mask_y, couplings[2]]


def stiffness(field, springs, ground):
    offsets = [1, GRID_X, GRID_X * GRID_Y]
    diag = ground
    for spring, step in zip(springs, offsets):
        diag = diag + (spring + behind(spring, step))
    result = diag * field
    for spring, step in zip(springs, offsets):
        result = result - spring * ahead(field, step) - behind(spring, step) * behind(field, step)
    return result


def precondition(resid, precond):
    count = resid.shape[0]
    blocks = resid.reshape(count, -1, BLK)
    out = jnp.einsum("cbj,bij->cbi", blocks, precond, precision=lax.Precision.HIGHEST)
    return out.reshape(count, -1)


def reference(forces, couplings, ground, precond):
    springs = spring_rows(couplings)
    modes = jnp.zeros_like(forces)
    resid = forces
    zvals = precondition(resid, precond)
    direction = zvals
    rz_now = jnp.sum(resid * zvals, axis=1)
    for step in range(ITERS):
        image = stiffness(direction, springs, ground)
        alpha = rz_now / jnp.sum(direction * image, axis=1)
        modes = modes + alpha[:, None] * direction
        resid = resid - alpha[:, None] * image
        if step + 1 < ITERS:
            zvals = precondition(resid, precond)
            rz_new = jnp.sum(resid * zvals, axis=1)
            direction = zvals + (rz_new / rz_now)[:, None] * direction
            rz_now = rz_new
    images = stiffness(modes, springs, ground)
    tile = jnp.dot(modes, images.T, precision=lax.Precision.HIGHEST) / NDOF
    return modes, tile
```

```python
import functools

import jax
import jax.numpy as jnp
from jax import lax
from jax.experimental import pallas as pl
from jax.experimental.pallas import tpu as pltpu
from jax.sharding import PartitionSpec as P

GRID_X = 32
GRID_Y = 32
PLANE = GRID_X * GRID_Y
LANES = 128
CHUNKS = PLANE // LANES
F32 = jnp.float32


def slot_planes():
    odd = lax.rem(lax.axis_index("nodes"), 2)
    return 1 - odd, odd


def split(x):
    high = x.astype(jnp.bfloat16)
    return high, (x - high.astype(F32)).astype(jnp.bfloat16)


def product(left, right, dims):
    left_high, left_low = left
    right_high, right_low = right
    dot = functools.partial(
        lax.dot_general, dimension_numbers=(dims, ((), ())), preferred_element_type=F32
    )
    return dot(left_high, right_high) + (
        dot(left_low, right_high) + dot(left_high, right_low)
    )


def block_product(x, matrix):
    return product(split(x), split(matrix), ((1,), (0,)))


def chunk(k):
    return slice(k * LANES, (k + 1) * LANES)


def plane_chunk(plane, k):
    return pl.ds(pl.multiple_of(plane * PLANE + k * LANES, LANES), LANES)


def lane_index(rows=8):
    return lax.broadcasted_iota(jnp.int32, (rows, LANES), 1)


def ahead_row(here, after):
    lane = lax.broadcasted_iota(jnp.int32, here.shape, here.ndim - 1)
    mixed = here if after is None else jnp.where(lane < GRID_X, after, here)
    return pltpu.roll(mixed, LANES - GRID_X, mixed.ndim - 1)


def behind_row(before, here):
    lane = lax.broadcasted_iota(jnp.int32, here.shape, here.ndim - 1)
    mixed = here if before is None else jnp.where(lane >= LANES - GRID_X, before, here)
    return pltpu.roll(mixed, GRID_X, mixed.ndim - 1)


def plane_springs(couplings, ground, plane, middle, crossing):
    lane = lane_index()
    inside_x = lane % GRID_X < GRID_X - 1

    def row(ref, index, k):
        return jnp.broadcast_to(ref[index : index + 1, plane_chunk(plane, k)], (8, LANES))

    along_y = []
    for k in range(CHUNKS):
        spring = row(couplings, 1, k)
        if k == CHUNKS - 1:
            spring = jnp.where(lane < LANES - GRID_X, spring, 0.0)
        along_y.append(spring)
    result = []
    for k in range(CHUNKS):
        right = jnp.where(inside_x, row(couplings, 0, k), 0.0)
        left = pltpu.roll(right, 1, 1)
        up = along_y[k]
        before = along_y[k - 1] if k else jnp.zeros_like(up)
        down = behind_row(before, up)
        diag = row(ground, 0, k) + (right + left) + (up + down) + (middle[k] + crossing[k])
        result.append((diag, right, left, up, down, middle[k], crossing[k]))
    return result


def all_springs(couplings, ground, got, rows):
    odd = lax.rem(lax.axis_index("nodes"), 2)
    own, mid = [], []
    for k in range(CHUNKS):
        own.append(jnp.broadcast_to(couplings[2:3, PLANE + k * LANES : PLANE + (k + 1) * LANES], (8, LANES)))
        mid.append(jnp.broadcast_to(couplings[2:3, chunk(k)], (8, LANES)))
    result = []
    for slot, plane in enumerate(slot_planes()):
        theirs = odd == (1 - slot)
        crossing = [
            jnp.where(theirs, got[slot][rows : rows + 8, chunk(k)], own[k])
            for k in range(CHUNKS)
        ]
        result.append(plane_springs(couplings, ground, plane, mid, crossing))
    return result


def stiff_chunk(springs, k, field, other, halo, rows):
    def load(ref, index):
        return ref[0:rows, chunk(index)].reshape(rows // 8, 8, LANES)

    diag, right, left, up, down, middle, crossing = springs[k]
    here = load(field, k)
    before = load(field, k - 1) if k else None
    after = load(field, k + 1) if k < CHUNKS - 1 else None
    result = diag * here
    result = result - right * pltpu.roll(here, LANES - 1, 2)
    result = result - left * pltpu.roll(here, 1, 2)
    result = result - up * ahead_row(here, after)
    result = result - down * behind_row(before, here)
    result = result - middle * load(other, k)
    result = result - crossing * load(halo, k)
    return result.reshape(rows, LANES)


def first_kernel(forces, couplings, precond, out_a, out_b):
    rows = forces.shape[0]
    for out, plane in zip((out_a, out_b), slot_planes()):
        for k in range(CHUNKS):
            out[0:rows, chunk(k)] = block_product(
                forces[:, plane_chunk(plane, k)], precond[plane * CHUNKS + k]
            )
            out[rows : rows + 8, chunk(k)] = jnp.broadcast_to(
                couplings[2:3, PLANE + k * LANES : PLANE + (k + 1) * LANES], (8, LANES)
            )


def other_kernel(forces, precond, out):
    for slot, plane in enumerate(slot_planes()):
        for k in range(CHUNKS):
            out[slot, :, chunk(k)] = block_product(
                forces[:, plane_chunk(plane, k)], precond[plane * CHUNKS + k]
            )


def second_kernel(couplings, ground, precond, d_a, d_b, got_a, got_b, q, w_a, w_b):
    rows = w_a.shape[0]
    springs = all_springs(couplings, ground, (got_a, got_b), rows)
    fields = (d_a, d_b)
    for slot, plane in enumerate(slot_planes()):
        for k in range(CHUNKS):
            image = stiff_chunk(
                springs[slot], k, fields[slot], fields[1 - slot], (got_a, got_b)[slot], rows
            )
            q[slot, :, chunk(k)] = image
            (w_a, w_b)[slot][:, chunk(k)] = block_product(
                image, precond[plane * CHUNKS + k]
            )


def third_kernel(forces, couplings, ground, d_a, d_b, got_a, got_b, q, w_a, w_b, next_a, next_b, v, dots):
    rows = w_a.shape[0]
    springs = all_springs(couplings, ground, (got_a, got_b), rows)
    fields = (w_a, w_b)
    sums = [jnp.zeros((rows, LANES), F32) for _ in range(4)]
    for slot, plane in enumerate(slot_planes()):
        for k in range(CHUNKS):
            image = stiff_chunk(
                springs[slot], k, fields[slot], fields[1 - slot], (next_a, next_b)[slot], rows
            )
            v[slot, :, chunk(k)] = image
            force = forces[:, plane_chunk(plane, k)]
            d_here = (d_a, d_b)[slot][0:rows, chunk(k)]
            q_here = q[slot, :, chunk(k)]
            w_here = fields[slot][:, chunk(k)]
            sums[0] += force * d_here
            sums[1] += d_here * q_here
            sums[2] += q_here * w_here
            sums[3] += w_here * image
    lane = lane_index(rows)
    packed = jnp.zeros((rows, LANES), F32)
    for index, value in enumerate(sums):
        packed = jnp.where(lane == index, jnp.sum(value, axis=1, keepdims=True), packed)
    if rows < LANES:
        packed = jnp.concatenate([packed, jnp.zeros((LANES - rows, LANES), F32)], axis=0)
    dots[...] = packed.T[0:8, :]


def fourth_kernel(n_dots, n_cols, exchange, *refs):
    dots, refs = refs[:n_dots], refs[n_dots:]
    d_a, d_b, q, v, refs = *refs[:4], refs[4:]
    d_all, refs = [(d_a, d_b)] + [tuple(refs[2 * i : 2 * i + 2]) for i in range(n_cols - 1)], refs[2 * n_cols - 2 :]
    w_all, refs = [tuple(refs[2 * i : 2 * i + 2]) for i in range(n_cols)], refs[2 * n_cols :]
    modes, coeffs, outs, gram = refs[0], refs[1], refs[2:-1], refs[-1]
    rows = modes.shape[0]
    total = dots[0][...]
    for piece in dots[1:]:
        total = total + piece[...]
    rz0, dq, qw, wv = (total[i : i + 1, :] for i in range(4))
    alpha0 = rz0 / dq
    rz1 = alpha0 * alpha0 * qw - rz0
    grow = 1.0 + rz1 / rz0
    curve1 = grow * grow * dq - 2.0 * alpha0 * grow * qw + alpha0 * alpha0 * wv
    alpha1 = rz1 / curve1
    used = lane_index(1) < rows
    on_d = jnp.where(used, alpha0 + alpha1 * grow, 0.0)
    on_w = jnp.where(used, -alpha0 * alpha1, 0.0)
    both = jnp.concatenate([on_d, on_w, jnp.zeros((LANES - 2, LANES), F32)], axis=0)
    coeffs[...] = both[0:8, :]
    turned = both.T
    p = jnp.broadcast_to(turned[0:rows, 0:1], (rows, LANES))
    s = jnp.broadcast_to(turned[0:rows, 1:2], (rows, LANES))
    sums = [None] * n_cols
    for slot, plane in enumerate(slot_planes()):
        high, low = [], []
        for k in range(CHUNKS):
            d_here = (d_a, d_b)[slot][0:rows, chunk(k)]
            w_here = w_all[0][slot][:, chunk(k)]
            modes[:, plane_chunk(plane, k)] = p * d_here + s * w_here
            image = p * q[slot, :, chunk(k)] + s * v[slot, :, chunk(k)]
            image_high, image_low = split(image)
            high.append(image_high)
            low.append(image_low)
        image = (jnp.concatenate(high, axis=1), jnp.concatenate(low, axis=1))
        for i in range(n_cols):
            columns = jnp.concatenate(
                [d_all[i][slot][0:rows, :], w_all[i][slot][0:rows, :]], axis=0
            )
            term = product(image, split(columns), ((1,), (1,)))
            sums[i] = term if sums[i] is None else sums[i] + term
    if exchange:
        for i in range(n_cols):
            gram[i] = sums[i]
        mine = lax.axis_index("nodes") ^ lax.axis_index("cols")
        for i in range(n_cols):
            outs[i][...] = gram[mine ^ i]
    else:
        for i in range(n_cols):
            outs[0][i] = sums[i]


def fifth_kernel(scale, n_sums, *refs):
    sums, coeffs, tile = refs[:n_sums], refs[n_sums], refs[n_sums + 1]
    rows = tile.shape[0]
    total = sums[0][...]
    for piece in sums[1:]:
        total = total + piece[...]
    tile[...] = (
        coeffs[0:1, 0:rows] * total[:, 0:rows] + coeffs[1:2, 0:rows] * total[:, rows : 2 * rows]
    ) * scale


def call(kernel, name, args, shapes, scratch=()):
    return pl.pallas_call(
        kernel,
        out_shape=[jax.ShapeDtypeStruct(shape, F32) for shape in shapes],
        in_specs=[pl.BlockSpec(memory_space=pltpu.VMEM)] * len(args),
        out_specs=[pl.BlockSpec(memory_space=pltpu.VMEM)] * len(shapes),
        scratch_shapes=scratch,
        name=name,
    )(*args)


def pairs(count, first):
    result = []
    for low in range(first, count - 1, 2):
        result += [(low, low + 1), (low + 1, low)]
    return result


def swapped(block, axis, bit):
    return lax.ppermute(block, axis, [(i, i ^ bit) for i in range(lax.axis_size(axis))])


def on_device(forces, couplings, ground, precond):
    rows, length = forces.shape
    nodes, cols = lax.axis_size("nodes"), lax.axis_size("cols")
    ground = ground.reshape(1, length)
    bits = []
    while 2 ** len(bits) < cols:
        bits.insert(0, 2 ** len(bits))

    def gathered(block, first=None):
        held = {0: block}
        for bit in bits:
            for key in list(held):
                held[key ^ bit] = swapped(held[key], "cols", bit)
        return held

    field = (rows, PLANE)
    d_a, d_b = call(
        first_kernel, "first", (forces, couplings, precond), [(rows + 8, PLANE)] * 2
    )
    got_a = lax.ppermute(d_a, "nodes", pairs(nodes, 0))
    got_b = lax.ppermute(d_b, "nodes", pairs(nodes, 1))
    d_held = {0: (d_a, d_b)}
    if bits:
        forces_far = swapped(forces, "cols", bits[0])
        (d_far,) = call(other_kernel, "other", (forces_far, precond), [(2, rows, PLANE)])
        d_held[bits[0]] = (d_far[0], d_far[1])
        for bit in bits[1:]:
            for key in list(d_held):
                d_held[key ^ bit] = tuple(swapped(x, "cols", bit) for x in d_held[key])
    q, w_a, w_b = call(
        second_kernel,
        "second",
        (couplings, ground, precond, d_a, d_b, got_a, got_b),
        [(2,) + field, field, field],
    )
    next_a = lax.ppermute(w_a, "nodes", pairs(nodes, 0))
    next_b = lax.ppermute(w_b, "nodes", pairs(nodes, 1))
    w_held_a, w_held_b = gathered(w_a), gathered(w_b)
    v, dots = call(
        third_kernel,
        "third",
        (forces, couplings, ground, d_a, d_b, got_a, got_b, q, w_a, w_b, next_a, next_b),
        [(2,) + field, (8, LANES)],
    )
    exchange = nodes == cols
    if exchange:
        dots = [dots] + [swapped(dots, "nodes", i) for i in range(1, nodes)]
    else:
        dots = [lax.psum(dots, "nodes")]
    operands = dots + [d_a, d_b, q, v]
    for i in range(1, cols):
        operands += d_held[i]
    for i in range(cols):
        operands += [w_held_a[i], w_held_b[i]]
    sums = [(rows, LANES)] * cols if exchange else [(cols, rows, LANES)]
    modes, coeffs, *grams = call(
        functools.partial(fourth_kernel, len(dots), cols, exchange),
        "fourth",
        operands,
        [(rows, length), (8, LANES)] + sums,
        [pltpu.VMEM((cols, rows, LANES), F32)],
    )
    scale = 1.0 / (length * nodes)
    if exchange:
        turn = [(n * cols + c, c * cols + n) for n in range(nodes) for c in range(cols)]
        theirs = lax.ppermute(coeffs, ("nodes", "cols"), turn)
        sums = [grams[0]] + [swapped(grams[i], "nodes", i) for i in range(1, nodes)]
        (tile,) = call(
            functools.partial(fifth_kernel, scale, nodes),
            "fifth",
            (*sums, theirs),
            [(rows, rows)],
        )
    else:
        gram = grams[0]
        every = lax.all_gather(coeffs, "cols")
        mine = lax.axis_index("cols")
        parts = []
        for i in range(cols):
            block = lax.dynamic_index_in_dim(gram, mine ^ i, 0, keepdims=False)
            parts.append(
                every[i, 0:1, 0:rows] * block[:, 0:rows]
                + every[i, 1:2, 0:rows] * block[:, rows : 2 * rows]
            )
        partial = jnp.concatenate(parts, axis=1) * scale
        tile = lax.psum_scatter(partial, "nodes", scatter_dimension=1, tiled=True)
    return (modes, tile)


def solution(mesh):
    in_specs = (
        P("cols", ("groups", "nodes")),
        P(None, ("groups", "nodes")),
        P(("groups", "nodes")),
        P(("groups", "nodes"), None, None),
    )
    out_specs = (P("cols", ("groups", "nodes")), P(("groups", "cols"), "nodes"))
    return jax.shard_map(
        on_device, mesh=mesh, in_specs=in_specs, out_specs=out_specs, check_vma=False
    )
```

```python
import functools

import jax
import jax.numpy as jnp
from jax import lax
from jax.experimental import pallas as pl
from jax.experimental.pallas import tpu as pltpu
from jax.sharding import PartitionSpec as P

GRID_X = 32
GRID_Y = 32
PLANE = GRID_X * GRID_Y
LANES = 128
CHUNKS = PLANE // LANES
F32 = jnp.float32
KERNEL_BYTES = 8 * 2**20


def slot_planes():
    odd = lax.rem(lax.axis_index("nodes"), 2)
    return 1 - odd, odd


def split(x):
    high = x.astype(jnp.bfloat16)
    return high, (x - high.astype(F32)).astype(jnp.bfloat16)


def product(left, right, dims):
    left_high, left_low = left
    right_high, right_low = right
    dot = functools.partial(
        lax.dot_general, dimension_numbers=(dims, ((), ())), preferred_element_type=F32
    )
    return dot(left_high, right_high) + (
        dot(left_low, right_high) + dot(left_high, right_low)
    )


def block_product(x, matrix):
    return product(split(x), split(matrix), ((1,), (0,)))


def chunk(k):
    return slice(k * LANES, (k + 1) * LANES)


def plane_chunk(plane, k):
    return pl.ds(pl.multiple_of(plane * PLANE + k * LANES, LANES), LANES)


def lane_index(rows=8):
    return lax.broadcasted_iota(jnp.int32, (rows, LANES), 1)


def ahead_row(here, after):
    lane = lax.broadcasted_iota(jnp.int32, here.shape, here.ndim - 1)
    mixed = here if after is None else jnp.where(lane < GRID_X, after, here)
    return pltpu.roll(mixed, LANES - GRID_X, mixed.ndim - 1)


def behind_row(before, here):
    lane = lax.broadcasted_iota(jnp.int32, here.shape, here.ndim - 1)
    mixed = here if before is None else jnp.where(lane >= LANES - GRID_X, before, here)
    return pltpu.roll(mixed, GRID_X, mixed.ndim - 1)


def plane_springs(couplings, ground, plane, middle, crossing, meets):
    lane = lane_index()
    inside_x = lane % GRID_X < GRID_X - 1

    def row(ref, index, k):
        return jnp.broadcast_to(ref[index : index + 1, plane_chunk(plane, k)], (8, LANES))

    along_y = []
    for k in range(CHUNKS):
        spring = row(couplings, 1, k)
        if k == CHUNKS - 1:
            spring = jnp.where(lane < LANES - GRID_X, spring, 0.0)
        along_y.append(spring)
    result = []
    for k in range(CHUNKS):
        right = jnp.where(inside_x, row(couplings, 0, k), 0.0)
        left = pltpu.roll(right, 1, 1)
        up = along_y[k]
        before = along_y[k - 1] if k else jnp.zeros_like(up)
        down = behind_row(before, up)
        diag = row(ground, 0, k) + (right + left) + (up + down) + (middle[k] + crossing[k])
        halo = jnp.where(meets, crossing[k], 0.0)
        result.append((diag, right, left, up, down, middle[k], halo))
    return result


def all_springs(couplings, ground, got, rows):
    place, count = lax.axis_index("nodes"), lax.axis_size("nodes")
    odd = lax.rem(place, 2)
    own, mid = [], []
    for k in range(CHUNKS):
        own.append(
            jnp.broadcast_to(
                couplings[2:3, PLANE + k * LANES : PLANE + (k + 1) * LANES], (8, LANES)
            )
        )
        mid.append(jnp.broadcast_to(couplings[2:3, chunk(k)], (8, LANES)))
    result = []
    for slot, plane in enumerate(slot_planes()):
        below = odd == (1 - slot)
        meets = jnp.where(below, place > 0, place < count - 1)
        crossing = [
            jnp.where(
                below,
                jnp.where(place > 0, got[slot][rows : rows + 8, chunk(k)], 0.0),
                own[k],
            )
            for k in range(CHUNKS)
        ]
        result.append(plane_springs(couplings, ground, plane, mid, crossing, meets))
    return result


def stiff_chunk(springs, k, field, other, halo, rows):
    def load(ref, index):
        return ref[0:rows, chunk(index)].reshape(rows // 8, 8, LANES)

    diag, right, left, up, down, middle, crossing = springs[k]
    here = load(field, k)
    before = load(field, k - 1) if k else None
    after = load(field, k + 1) if k < CHUNKS - 1 else None
    result = diag * here
    result = result - right * pltpu.roll(here, LANES - 1, 2)
    result = result - left * pltpu.roll(here, 1, 2)
    result = result - up * ahead_row(here, after)
    result = result - down * behind_row(before, here)
    result = result - middle * load(other, k)
    result = result - crossing * load(halo, k)
    return result.reshape(rows, LANES)


def first_kernel(forces, couplings, precond, out_a, out_b, field, matrices, springs, sems):
    rows = forces.shape[0]
    copies = []
    for slot, plane in enumerate(slot_planes()):
        here = pl.ds(pl.multiple_of(plane * PLANE, PLANE), PLANE)
        copies.append(
            (
                pltpu.make_async_copy(forces.at[:, here], field.at[slot], sems.at[slot, 0]),
                pltpu.make_async_copy(
                    precond.at[pl.ds(plane * CHUNKS, CHUNKS)], matrices.at[slot], sems.at[slot, 1]
                ),
            )
        )
    spring_copy = pltpu.make_async_copy(couplings, springs, sems.at[2, 0])
    for pair in copies:
        for copy in pair:
            copy.start()
    spring_copy.start()
    for slot, out in enumerate((out_a, out_b)):
        for copy in copies[slot]:
            copy.wait()
        for k in range(CHUNKS):
            out[0:rows, chunk(k)] = block_product(field[slot, :, chunk(k)], matrices[slot, k])
    spring_copy.wait()
    for out in (out_a, out_b):
        for k in range(CHUNKS):
            out[rows : rows + 8, chunk(k)] = jnp.broadcast_to(
                springs[2:3, PLANE + k * LANES : PLANE + (k + 1) * LANES], (8, LANES)
            )


def other_kernel(forces, precond, out):
    for slot, plane in enumerate(slot_planes()):
        for k in range(CHUNKS):
            out[slot, :, chunk(k)] = block_product(
                forces[:, plane_chunk(plane, k)], precond[plane * CHUNKS + k]
            )


def second_kernel(couplings, ground, precond, d_a, d_b, got_a, got_b, q, w_a, w_b, near):
    rows = w_a.shape[0]
    springs = all_springs(couplings, ground, (got_a, got_b), rows)
    fields = (d_a, d_b)
    for slot, plane in enumerate(slot_planes()):
        for k in range(CHUNKS):
            image = stiff_chunk(
                springs[slot], k, fields[slot], fields[1 - slot], (got_a, got_b)[slot], rows
            )
            q[slot, :, chunk(k)] = image
            w = block_product(image, precond[plane * CHUNKS + k])
            (w_a, w_b)[slot][:, chunk(k)] = w
            near[slot, 0:rows, chunk(k)] = fields[slot][0:rows, chunk(k)]
            near[slot, rows : 2 * rows, chunk(k)] = w


def place_sums(packed, first, sums):
    lane = lane_index(packed.shape[0])
    for index, value in enumerate(sums):
        total = jnp.sum(value, axis=1, keepdims=True)
        packed = jnp.where(lane == first + index, total, packed)
    return packed


def side_kernel(forces, q, near, packed):
    rows = forces.shape[0]
    sums = [jnp.zeros((rows, LANES), F32) for _ in range(3)]
    for slot, plane in enumerate(slot_planes()):
        for k in range(CHUNKS):
            d_here = near[slot, 0:rows, chunk(k)]
            q_here = q[slot, :, chunk(k)]
            sums[0] += forces[:, plane_chunk(plane, k)] * d_here
            sums[1] += d_here * q_here
            sums[2] += q_here * near[slot, rows : 2 * rows, chunk(k)]
    packed[...] = place_sums(jnp.zeros((rows, LANES), F32), 0, sums)


def third_kernel(couplings, ground, got_a, got_b, w_a, w_b, next_a, next_b, packed, v, dots):
    rows = w_a.shape[0]
    springs = all_springs(couplings, ground, (got_a, got_b), rows)
    fields = (w_a, w_b)
    total = jnp.zeros((rows, LANES), F32)
    for slot in range(2):
        for k in range(CHUNKS):
            image = stiff_chunk(
                springs[slot], k, fields[slot], fields[1 - slot], (next_a, next_b)[slot], rows
            )
            v[slot, :, chunk(k)] = image
            total += fields[slot][:, chunk(k)] * image
    values = place_sums(packed[...], 3, [total])
    if rows < LANES:
        values = jnp.concatenate([values, jnp.zeros((LANES - rows, LANES), F32)], axis=0)
    dots[...] = values.T[0:8, :]


def columns_of(field, slot, rows):
    return jnp.concatenate([part[slot, 0:rows, :] for part in field], axis=0)


def early_kernel(n_near, n_far, q, v, *refs):
    near, d_far = refs[:n_near], refs[n_near : n_near + n_far]
    qv_high, qv_low, near_gram, far_gram = refs[n_near + n_far :]
    rows = q.shape[1]
    near_sums, far_sum = [None] * n_near, None
    for slot in range(2):
        images = split(jnp.concatenate([q[slot], v[slot]], axis=0))
        qv_high[slot], qv_low[slot] = images
        for i in range(n_near):
            term = product(images, split(near[i][slot]), ((1,), (1,)))
            near_sums[i] = term if slot == 0 else near_sums[i] + term
        term = product(images, split(columns_of(d_far, slot, rows)), ((1,), (1,)))
        far_sum = term if slot == 0 else far_sum + term
    for i in range(n_near):
        near_gram[i] = near_sums[i]
    far_gram[...] = far_sum


def late_kernel(n_dots, n_near, n_far, exchange, *refs):
    dots, refs = refs[:n_dots], refs[n_dots:]
    qv_high, qv_low, near_gram, far_gram, refs = *refs[:4], refs[4:]
    w_far, coeffs, outs, gram = refs[: 2 * n_far], refs[2 * n_far], refs[2 * n_far + 1 : -1], refs[-1]
    rows = near_gram.shape[1] // 2
    far_sum = None
    for slot in range(2):
        columns = jnp.concatenate([w_far[2 * i + slot][...] for i in range(n_far)], axis=0)
        term = product((qv_high[slot], qv_low[slot]), split(columns), ((1,), (1,)))
        far_sum = term if slot == 0 else far_sum + term
    total = dots[0][...]
    for piece in dots[1:]:
        total = total + piece[...]
    rz0, dq, qw, wv = (total[i : i + 1, :] for i in range(4))
    alpha0 = rz0 / dq
    rz1 = alpha0 * alpha0 * qw - rz0
    grow = 1.0 + rz1 / rz0
    curve1 = grow * grow * dq - 2.0 * alpha0 * grow * qw + alpha0 * alpha0 * wv
    alpha1 = rz1 / curve1
    used = lane_index(1) < rows
    on_d = jnp.where(used, alpha0 + alpha1 * grow, 0.0)
    on_w = jnp.where(used, -alpha0 * alpha1, 0.0)
    coeffs[...] = jnp.concatenate([on_d, on_w, jnp.zeros((6, LANES), F32)], axis=0)
    p, s = turned(coeffs, rows)
    if not exchange:
        gram = outs[0]
    for i in range(n_near):
        gram[i] = p * near_gram[i, 0:rows] + s * near_gram[i, rows : 2 * rows]
    d_part, w_part = far_gram[...], far_sum
    for i in range(n_far):
        there = slice(i * rows, (i + 1) * rows)
        both = jnp.concatenate([d_part[:, there], w_part[:, there]], axis=1)
        gram[n_near + i] = p * both[0:rows] + s * both[rows : 2 * rows]
    if exchange:
        mine = lax.axis_index("nodes") ^ lax.axis_index("cols")
        for i in range(n_near + n_far):
            outs[i][...] = gram[mine ^ i]


def turned(coeffs, rows):
    table = jnp.concatenate([coeffs[...], jnp.zeros((LANES - 8, LANES), F32)], axis=0).T
    return [jnp.broadcast_to(table[0:rows, i : i + 1], (rows, LANES)) for i in range(2)]


def modes_kernel(coeffs, near, modes):
    rows = modes.shape[0]
    p, s = turned(coeffs, rows)
    for slot, plane in enumerate(slot_planes()):
        for k in range(CHUNKS):
            modes[:, plane_chunk(plane, k)] = (
                p * near[slot, 0:rows, chunk(k)] + s * near[slot, rows : 2 * rows, chunk(k)]
            )


def fifth_kernel(scale, n_sums, *refs):
    sums, own, theirs, tile = refs[:n_sums], refs[n_sums], refs[n_sums + 1], refs[n_sums + 2]
    rows = tile.shape[0]
    total = sums[0][...]
    for piece in sums[1:]:
        total = total + piece[...]
    here = lax.axis_index("nodes") == lax.axis_index("cols")
    coeffs = jnp.where(here, own[...], theirs[...])
    tile[...] = (
        coeffs[0:1, 0:rows] * total[:, 0:rows] + coeffs[1:2, 0:rows] * total[:, rows : 2 * rows]
    ) * scale


def call(kernel, name, args, shapes, scratch=(), space=pltpu.VMEM):
    shapes = [
        shape if isinstance(shape, jax.ShapeDtypeStruct) else jax.ShapeDtypeStruct(shape, F32)
        for shape in shapes
    ]
    return pl.pallas_call(
        kernel,
        out_shape=shapes,
        in_specs=[pl.BlockSpec(memory_space=space)] * len(args),
        out_specs=[pl.BlockSpec(memory_space=pltpu.VMEM)] * len(shapes),
        scratch_shapes=scratch,
        compiler_params=pltpu.CompilerParams(vmem_limit_bytes=KERNEL_BYTES),
        name=name,
    )(*args)


def neighbours(block, first):
    nodes, cols = lax.axis_size("nodes"), lax.axis_size("cols")
    route = []
    for n in range(nodes):
        other = n + 1 if n % 2 == first else n - 1
        for c in range(cols):
            here = n * cols + c
            if 0 <= other < nodes:
                route.append((here, other * cols + c))
            elif cols % 2 == 0:
                route.append((here, here ^ 1))
    return lax.ppermute(block, ("nodes", "cols"), route)


def transposed(block):
    nodes, cols = lax.axis_size("nodes"), lax.axis_size("cols")
    route = []
    for n in range(nodes):
        for c in range(cols):
            there = c * cols + n if n != c else (n ^ 1) * (cols + 1)
            route.append((n * cols + c, there))
    return lax.ppermute(block, ("nodes", "cols"), route)


def swapped(block, axis, bit):
    return lax.ppermute(block, axis, [(i, i ^ bit) for i in range(lax.axis_size(axis))])


def on_device(forces, couplings, ground, precond):
    rows, length = forces.shape
    nodes, cols = lax.axis_size("nodes"), lax.axis_size("cols")
    ground = ground.reshape(1, length)
    bits = []
    while 2 ** len(bits) < cols:
        bits.append(2 ** len(bits))
    top = cols // 2

    def shared(block):
        held = {0: block}
        for bit in bits[:-1]:
            for key in list(held):
                held[key ^ bit] = swapped(held[key], "cols", bit)
        return [held[key] for key in range(max(top, 1))]

    field = (rows, PLANE)
    d_a, d_b = call(
        first_kernel,
        "first",
        (forces, couplings, precond),
        [(rows + 8, PLANE)] * 2,
        [
            pltpu.VMEM((2, rows, PLANE), F32),
            pltpu.VMEM((2, CHUNKS, LANES, LANES), F32),
            pltpu.VMEM(couplings.shape, F32),
            pltpu.SemaphoreType.DMA((3, 2)),
        ],
        pl.ANY,
    )
    got_a, got_b = neighbours(d_a, 0), neighbours(d_b, 1)
    forces_far = swapped(forces, "cols", top)
    got_a, got_b, forces_far = lax.optimization_barrier((got_a, got_b, forces_far))
    q, w_a, w_b, near = call(
        second_kernel,
        "second",
        (couplings, ground, precond, d_a, d_b, got_a, got_b),
        [(2,) + field, field, field, (2, 2 * rows, PLANE)],
    )
    next_a, next_b = neighbours(w_a, 0), neighbours(w_b, 1)
    w_far_a, w_far_b = swapped(w_a, "cols", top), swapped(w_b, "cols", top)
    near = shared(near)
    (d_far,) = call(other_kernel, "other", (forces_far, precond), [(2,) + field])
    d_far = shared(d_far)
    (packed,) = call(side_kernel, "side", (forces, q, near[0]), [(rows, LANES)])
    next_a, next_b, near, d_far, packed = lax.optimization_barrier(
        (next_a, next_b, near, d_far, packed)
    )
    v, dots = call(
        third_kernel,
        "third",
        (couplings, ground, got_a, got_b, w_a, w_b, next_a, next_b, packed),
        [(2,) + field, (8, LANES)],
    )
    exchange = nodes == cols
    if exchange:
        dots = [dots] + [swapped(dots, "nodes", i) for i in range(1, nodes)]
    else:
        dots = [lax.psum(dots, "nodes")]
    halves = jax.ShapeDtypeStruct((2, 2 * rows, PLANE), jnp.bfloat16)
    qv_high, qv_low, near_gram, far_gram = call(
        functools.partial(early_kernel, len(near), len(d_far)),
        "early",
        (q, v, *near, *d_far),
        [halves, halves, (len(near), 2 * rows, 2 * rows), (2 * rows, len(d_far) * rows)],
    )
    w_far_a, w_far_b, near_gram, *dots = lax.optimization_barrier(
        (w_far_a, w_far_b, near_gram, *dots)
    )
    w_far = [x for pair in zip(shared(w_far_a), shared(w_far_b)) for x in pair]
    coeffs, *grams = call(
        functools.partial(late_kernel, len(dots), len(near), len(d_far), exchange),
        "late",
        (*dots, qv_high, qv_low, near_gram, far_gram, *w_far),
        [(8, LANES)] + ([(rows, LANES)] * cols if exchange else [(cols, rows, LANES)]),
        [pltpu.VMEM((cols, rows, LANES), F32)],
    )
    (modes,) = call(modes_kernel, "modes", (coeffs, near[0]), [(rows, length)])
    scale = 1.0 / (length * nodes)
    if exchange:
        theirs = transposed(coeffs)
        sums = [grams[0]] + [swapped(grams[i], "nodes", i) for i in range(1, nodes)]
        (tile,) = call(
            functools.partial(fifth_kernel, scale, nodes),
            "fifth",
            (*sums, coeffs, theirs),
            [(rows, rows)],
        )
    else:
        gram = grams[0]
        every = lax.all_gather(coeffs, "cols")
        mine = lax.axis_index("cols")
        parts = []
        for i in range(cols):
            block = lax.dynamic_index_in_dim(gram, mine ^ i, 0, keepdims=False)
            parts.append(
                every[i, 0:1, 0:rows] * block[:, 0:rows]
                + every[i, 1:2, 0:rows] * block[:, rows : 2 * rows]
            )
        partial = jnp.concatenate(parts, axis=1) * scale
        tile = lax.psum_scatter(partial, "nodes", scatter_dimension=1, tiled=True)
    return (modes, tile)


def solution(mesh):
    in_specs = (
        P("cols", ("groups", "nodes")),
        P(None, ("groups", "nodes")),
        P(("groups", "nodes")),
        P(("groups", "nodes"), None, None),
    )
    out_specs = (P("cols", ("groups", "nodes")), P(("groups", "cols"), "nodes"))
    return jax.shard_map(
        on_device, mesh=mesh, in_specs=in_specs, out_specs=out_specs, check_vma=False
    )
```

```python
import functools

import jax
import jax.numpy as jnp
from jax import lax
from jax.experimental import pallas as pl
from jax.experimental.pallas import tpu as pltpu
from jax.sharding import PartitionSpec as P

GRID_X = 32
GRID_Y = 32
PLANE = GRID_X * GRID_Y
LANES = 128
CHUNKS = PLANE // LANES
F32 = jnp.float32
KERNEL_BYTES = 8 * 2**20


def slot_planes():
    odd = lax.rem(lax.axis_index("nodes"), 2)
    return odd, 1 - odd


def split(x):
    high = x.astype(jnp.bfloat16)
    return high, (x - high.astype(F32)).astype(jnp.bfloat16)


def product(left, right, dims):
    left_high, left_low = left
    right_high, right_low = right
    dot = functools.partial(
        lax.dot_general, dimension_numbers=(dims, ((), ())), preferred_element_type=F32
    )
    return dot(left_high, right_high) + (
        dot(left_low, right_high) + dot(left_high, right_low)
    )


def block_product(x, matrix):
    return product(split(x), split(matrix), ((1,), (0,)))


def chunk(k):
    return slice(k * LANES, (k + 1) * LANES)


def plane_chunk(plane, k):
    return pl.ds(pl.multiple_of(plane * PLANE + k * LANES, LANES), LANES)


def lane_index(rows=8):
    return lax.broadcasted_iota(jnp.int32, (rows, LANES), 1)


def ahead_row(here, after):
    lane = lax.broadcasted_iota(jnp.int32, here.shape, here.ndim - 1)
    mixed = here if after is None else jnp.where(lane < GRID_X, after, here)
    return pltpu.roll(mixed, LANES - GRID_X, mixed.ndim - 1)


def behind_row(before, here):
    lane = lax.broadcasted_iota(jnp.int32, here.shape, here.ndim - 1)
    mixed = here if before is None else jnp.where(lane >= LANES - GRID_X, before, here)
    return pltpu.roll(mixed, GRID_X, mixed.ndim - 1)


def plane_springs(couplings, ground, plane, middle, crossing, meets):
    lane = lane_index()
    inside_x = lane % GRID_X < GRID_X - 1

    def row(ref, index, k):
        return jnp.broadcast_to(ref[index : index + 1, plane_chunk(plane, k)], (8, LANES))

    along_y = []
    for k in range(CHUNKS):
        spring = row(couplings, 1, k)
        if k == CHUNKS - 1:
            spring = jnp.where(lane < LANES - GRID_X, spring, 0.0)
        along_y.append(spring)
    result = []
    for k in range(CHUNKS):
        right = jnp.where(inside_x, row(couplings, 0, k), 0.0)
        left = pltpu.roll(right, 1, 1)
        up = along_y[k]
        before = along_y[k - 1] if k else jnp.zeros_like(up)
        down = behind_row(before, up)
        diag = row(ground, 0, k) + (right + left) + (up + down) + (middle[k] + crossing[k])
        halo = jnp.where(meets, crossing[k], 0.0)
        result.append((diag, right, left, up, down, middle[k], halo))
    return result


def all_springs(couplings, ground, got):
    def row_before(slot, k):
        return jnp.broadcast_to(got[slot][0:1, chunk(k)], (8, LANES))

    place, count = lax.axis_index("nodes"), lax.axis_size("nodes")
    odd = lax.rem(place, 2)
    own, mid = [], []
    for k in range(CHUNKS):
        own.append(
            jnp.broadcast_to(
                couplings[2:3, PLANE + k * LANES : PLANE + (k + 1) * LANES], (8, LANES)
            )
        )
        mid.append(jnp.broadcast_to(couplings[2:3, chunk(k)], (8, LANES)))
    result = []
    for slot, plane in enumerate(slot_planes()):
        below = odd == slot
        meets = jnp.where(below, place > 0, place < count - 1)
        crossing = [
            jnp.where(
                below,
                jnp.where(place > 0, row_before(slot, k), 0.0),
                own[k],
            )
            for k in range(CHUNKS)
        ]
        result.append(plane_springs(couplings, ground, plane, mid, crossing, meets))
    return result


def stiff_chunk(springs, k, field, other, halo, rows):
    def load(ref, index):
        return ref[0:rows, chunk(index)].reshape(rows // 8, 8, LANES)

    diag, right, left, up, down, middle, crossing = springs[k]
    here = load(field, k)
    before = load(field, k - 1) if k else None
    after = load(field, k + 1) if k < CHUNKS - 1 else None
    result = diag * here
    result = result - right * pltpu.roll(here, LANES - 1, 2)
    result = result - left * pltpu.roll(here, 1, 2)
    result = result - up * ahead_row(here, after)
    result = result - down * behind_row(before, here)
    result = result - middle * load(other, k)
    result = result - crossing * load(halo, k)
    return result.reshape(rows, LANES)


def first_kernel(forces, precond, out_a, out_b, first_rows, field, matrices, sems):
    early = first_rows.shape[1]
    copies = []
    for slot, plane in enumerate(slot_planes()):
        here = pl.ds(pl.multiple_of(plane * PLANE, PLANE), PLANE)
        copies.append(
            (
                pltpu.make_async_copy(forces.at[:, here], field.at[slot], sems.at[slot, 0]),
                pltpu.make_async_copy(
                    precond.at[pl.ds(plane * CHUNKS, CHUNKS)], matrices.at[slot], sems.at[slot, 1]
                ),
            )
        )
    for pair in copies:
        for copy in pair:
            copy.start()
    for slot, out in enumerate((out_a, out_b)):
        for copy in copies[slot]:
            copy.wait()
        for k in range(CHUNKS):
            d = block_product(field[slot, :, chunk(k)], matrices[slot, k])
            out[:, chunk(k)] = d
            first_rows[slot, :, chunk(k)] = d[0:early]


def second_kernel(couplings, ground, before_a, before_b, precond, d_a, d_b, got_a, got_b, q, w_a, w_b, beside, near):
    rows = w_a.shape[0]
    early = 2 * rows - beside.shape[1]
    springs = all_springs(couplings, ground, (before_a, before_b))
    fields = (d_a, d_b)
    for slot, plane in enumerate(slot_planes()):
        for k in range(CHUNKS):
            image = stiff_chunk(
                springs[slot], k, fields[slot], fields[1 - slot], (got_a, got_b)[slot], rows
            )
            q[slot, :, chunk(k)] = image
            w = block_product(image, precond[plane * CHUNKS + k])
            (w_a, w_b)[slot][:, chunk(k)] = w
            beside[slot, 0:rows, chunk(k)] = w
            beside[slot, rows:, chunk(k)] = fields[slot][early:, chunk(k)]
            near[slot, 0:rows, chunk(k)] = fields[slot][:, chunk(k)]
            near[slot, rows : 2 * rows, chunk(k)] = w


def place_sums(packed, first, sums):
    lane = lane_index(packed.shape[0])
    for index, value in enumerate(sums):
        total = jnp.sum(value, axis=1, keepdims=True)
        packed = jnp.where(lane == first + index, total, packed)
    return packed


def side_kernel(forces, q, near, packed):
    rows = forces.shape[0]
    sums = [jnp.zeros((rows, LANES), F32) for _ in range(3)]
    for slot, plane in enumerate(slot_planes()):
        for k in range(CHUNKS):
            d_here = near[slot, 0:rows, chunk(k)]
            q_here = q[slot, :, chunk(k)]
            sums[0] += forces[:, plane_chunk(plane, k)] * d_here
            sums[1] += d_here * q_here
            sums[2] += q_here * near[slot, rows : 2 * rows, chunk(k)]
    packed[...] = place_sums(jnp.zeros((rows, LANES), F32), 0, sums)


def third_kernel(couplings, ground, before_a, before_b, w_a, w_b, next_a, next_b, packed, v, dots):
    rows = w_a.shape[0]
    springs = all_springs(couplings, ground, (before_a, before_b))
    fields = (w_a, w_b)
    total = jnp.zeros((rows, LANES), F32)
    for slot in range(2):
        for k in range(CHUNKS):
            image = stiff_chunk(
                springs[slot], k, fields[slot], fields[1 - slot], (next_a, next_b)[slot], rows
            )
            v[slot, :, chunk(k)] = image
            total += fields[slot][:, chunk(k)] * image
    values = place_sums(packed[...], 3, [total])
    if rows < LANES:
        values = jnp.concatenate([values, jnp.zeros((LANES - rows, LANES), F32)], axis=0)
    dots[...] = values.T[0:8, :]


def columns_of(fields, slot):
    return jnp.concatenate([field[slot] for field in fields], axis=0)


def early_kernel(n_near, n_far, q, v, *refs):
    near, d_far = refs[:n_near], refs[n_near : n_near + n_far]
    qv_high, qv_low, near_gram, far_gram = refs[n_near + n_far :]
    rows = q.shape[1]
    near_sums, far_sum = [None] * n_near, None
    for slot in range(2):
        images = split(jnp.concatenate([q[slot], v[slot]], axis=0))
        qv_high[slot], qv_low[slot] = images
        for i in range(n_near):
            term = product(images, split(near[i][slot]), ((1,), (1,)))
            near_sums[i] = term if slot == 0 else near_sums[i] + term
        term = product(images, split(columns_of(d_far, slot)), ((1,), (1,)))
        far_sum = term if slot == 0 else far_sum + term
    for i in range(n_near):
        near_gram[i] = near_sums[i]
    far_gram[...] = far_sum


def coeffs_kernel(rows, *refs):
    dots, coeffs = refs[:-1], refs[-1]
    total = dots[0][...]
    for piece in dots[1:]:
        total = total + piece[...]
    rz0, dq, qw, wv = (total[i : i + 1, :] for i in range(4))
    alpha0 = rz0 / dq
    rz1 = alpha0 * alpha0 * qw - rz0
    grow = 1.0 + rz1 / rz0
    curve1 = grow * grow * dq - 2.0 * alpha0 * grow * qw + alpha0 * alpha0 * wv
    alpha1 = rz1 / curve1
    used = lane_index(1) < rows
    on_d = jnp.where(used, alpha0 + alpha1 * grow, 0.0)
    on_w = jnp.where(used, -alpha0 * alpha1, 0.0)
    pair = jnp.concatenate([on_d, on_w, jnp.zeros((6, LANES), F32)], axis=0)
    for i in range(coeffs.shape[0] // 8):
        coeffs[8 * i : 8 * i + 8, :] = pair


def late_kernel(n_near, n_far, exchange, coeffs, qv_high, qv_low, near_gram, far_gram, *refs):
    far, outs, gram = refs[:n_far], refs[n_far:-1], refs[-1]
    rows = near_gram.shape[1] // 2
    far_sum = None
    for slot in range(2):
        images = (qv_high[slot], qv_low[slot])
        term = product(images, split(columns_of(far, slot)), ((1,), (1,)))
        far_sum = term if slot == 0 else far_sum + term
    p, s = turned(coeffs, rows)
    if not exchange:
        gram = outs[0]
    for i in range(n_near):
        gram[i] = p * near_gram[i, 0:rows] + s * near_gram[i, rows : 2 * rows]
    first_part = far_gram[...]
    early, width = first_part.shape[1] // n_far, far[0].shape[1]
    for i in range(n_far):
        both = jnp.concatenate(
            [
                first_part[:, i * early : (i + 1) * early],
                far_sum[:, i * width + rows : (i + 1) * width],
                far_sum[:, i * width : i * width + rows],
            ],
            axis=1,
        )
        gram[n_near + i] = p * both[0:rows] + s * both[rows : 2 * rows]
    if exchange:
        mine = lax.axis_index("nodes") ^ lax.axis_index("cols")
        for i in range(n_near + n_far):
            outs[i][...] = gram[mine ^ i]


def turned(coeffs, rows):
    table = jnp.concatenate([coeffs[0:8, :], jnp.zeros((LANES - 8, LANES), F32)], axis=0).T
    return [jnp.broadcast_to(table[0:rows, i : i + 1], (rows, LANES)) for i in range(2)]


def modes_kernel(coeffs, near, modes):
    rows = modes.shape[0]
    p, s = turned(coeffs, rows)
    for slot, plane in enumerate(slot_planes()):
        for k in range(CHUNKS):
            modes[:, plane_chunk(plane, k)] = (
                p * near[slot, 0:rows, chunk(k)] + s * near[slot, rows : 2 * rows, chunk(k)]
            )


def fifth_kernel(scale, n_sums, *refs):
    sums, own, theirs, tile = refs[:n_sums], refs[n_sums], refs[n_sums + 1], refs[n_sums + 2]
    rows = tile.shape[0]
    total = sums[0][...]
    for piece in sums[1:]:
        total = total + piece[...]
    here = lax.axis_index("nodes") == lax.axis_index("cols")
    coeffs = jnp.where(here, own[0:8, :], theirs[0:8, :])
    tile[...] = (
        coeffs[0:1, 0:rows] * total[:, 0:rows] + coeffs[1:2, 0:rows] * total[:, rows : 2 * rows]
    ) * scale


def call(kernel, name, args, shapes, scratch=(), space=pltpu.VMEM):
    shapes = [
        shape if isinstance(shape, jax.ShapeDtypeStruct) else jax.ShapeDtypeStruct(shape, F32)
        for shape in shapes
    ]
    return pl.pallas_call(
        kernel,
        out_shape=shapes,
        in_specs=[pl.BlockSpec(memory_space=space)] * len(args),
        out_specs=[pl.BlockSpec(memory_space=pltpu.VMEM)] * len(shapes),
        scratch_shapes=scratch,
        compiler_params=pltpu.CompilerParams(vmem_limit_bytes=KERNEL_BYTES),
        name=name,
    )(*args)


def neighbours(block, first):
    nodes, cols = lax.axis_size("nodes"), lax.axis_size("cols")
    route = []
    for n in range(nodes):
        other = n + 1 if n % 2 == first else n - 1
        for c in range(cols):
            here = n * cols + c
            if 0 <= other < nodes:
                route.append((here, other * cols + c))
            elif cols % 2 == 0:
                route.append((here, here ^ 1))
    return lax.ppermute(block, ("nodes", "cols"), route)


def transposed(block):
    nodes, cols = lax.axis_size("nodes"), lax.axis_size("cols")
    route = []
    for n in range(nodes):
        for c in range(cols):
            there = c * cols + n if n != c else (n ^ 1) * (cols + 1)
            route.append((n * cols + c, there))
    return lax.ppermute(block, ("nodes", "cols"), route)


def swapped(block, axis, bit):
    return lax.ppermute(block, axis, [(i, i ^ bit) for i in range(lax.axis_size(axis))])


def on_device(forces, couplings, ground, precond):
    rows, length = forces.shape
    nodes, cols = lax.axis_size("nodes"), lax.axis_size("cols")
    ground = ground.reshape(1, length)
    bits = []
    while 2 ** len(bits) < cols:
        bits.append(2 ** len(bits))
    top = cols // 2

    def shared(block):
        held = {0: block}
        for bit in bits[:-1]:
            for key in list(held):
                held[key ^ bit] = swapped(held[key], "cols", bit)
        return [held[key] for key in range(max(top, 1))]

    field = (rows, PLANE)
    early = rows * 3 // 4
    d_a, d_b, d_far = call(
        first_kernel,
        "first",
        [pltpu.with_memory_space_constraint(x, pltpu.HBM) for x in (forces, precond)],
        [field, field, (2, early, PLANE)],
        [
            pltpu.VMEM((2, rows, PLANE), F32),
            pltpu.VMEM((2, CHUNKS, LANES, LANES), F32),
            pltpu.SemaphoreType.DMA((2, 2)),
        ],
        pltpu.HBM,
    )
    got_a, got_b = neighbours(d_a, 1), neighbours(d_b, 0)
    d_far = swapped(d_far, "cols", top)
    last = couplings[2:3, length - PLANE :]
    before_a, before_b = neighbours(last, 1), neighbours(last, 0)
    got_a, got_b, d_far = lax.optimization_barrier((got_a, got_b, d_far))
    edges = (couplings, ground, before_a, before_b)
    q, w_a, w_b, beside, near = call(
        second_kernel,
        "second",
        (*edges, precond, d_a, d_b, got_a, got_b),
        [(2,) + field, field, field, (2, 2 * rows - early, PLANE), (2, 2 * rows, PLANE)],
    )
    next_a, next_b = neighbours(w_a, 1), neighbours(w_b, 0)
    far = swapped(beside, "cols", top)
    near = shared(near)
    next_a, next_b, d_far, near = lax.optimization_barrier((next_a, next_b, d_far, near))
    d_far = shared(d_far)
    (packed,) = call(side_kernel, "side", (forces, q, near[0]), [(rows, LANES)])
    v, dots = call(
        third_kernel,
        "third",
        (*edges, w_a, w_b, next_a, next_b, packed),
        [(2,) + field, (8, LANES)],
    )
    exchange = nodes == cols
    if exchange:
        dots = [dots] + [swapped(dots, "nodes", i) for i in reversed(range(1, nodes))]
    else:
        dots = [lax.psum(dots, "nodes")]
    halves = jax.ShapeDtypeStruct((2, 2 * rows, PLANE), jnp.bfloat16)
    qv_high, qv_low, near_gram, far_gram = call(
        functools.partial(early_kernel, len(near), len(d_far)),
        "early",
        (q, v, *near, *d_far),
        [halves, halves, (len(near), 2 * rows, 2 * rows), (2 * rows, len(d_far) * early)],
    )
    far, near_gram, *dots = lax.optimization_barrier((far, near_gram, *dots))
    far = shared(far)
    (coeffs,) = call(functools.partial(coeffs_kernel, rows), "coeffs", dots, [(rows + 8, LANES)])
    grams = call(
        functools.partial(late_kernel, len(near), len(d_far), exchange),
        "late",
        (coeffs, qv_high, qv_low, near_gram, far_gram, *far),
        [(rows, LANES)] * cols if exchange else [(cols, rows, LANES)],
        [pltpu.VMEM((cols, rows, LANES), F32)],
    )
    scale = 1.0 / (length * nodes)
    (modes,) = call(modes_kernel, "modes", (coeffs, near[0]), [(rows, length)])
    if exchange:
        theirs = transposed(coeffs)
        sums = [grams[0]] + [swapped(grams[i], "nodes", i) for i in reversed(range(1, nodes))]
        (tile,) = call(
            functools.partial(fifth_kernel, scale, nodes),
            "fifth",
            (*sums, coeffs, theirs),
            [(rows, rows)],
        )
    else:
        gram = grams[0]
        every = lax.all_gather(coeffs, "cols")
        mine = lax.axis_index("cols")
        parts = []
        for i in range(cols):
            block = lax.dynamic_index_in_dim(gram, mine ^ i, 0, keepdims=False)
            parts.append(
                every[i, 0:1, 0:rows] * block[:, 0:rows]
                + every[i, 1:2, 0:rows] * block[:, rows : 2 * rows]
            )
        partial = jnp.concatenate(parts, axis=1) * scale
        tile = lax.psum_scatter(partial, "nodes", scatter_dimension=1, tiled=True)
    return (modes, tile)


def solution(mesh):
    in_specs = (
        P("cols", ("groups", "nodes")),
        P(None, ("groups", "nodes")),
        P(("groups", "nodes")),
        P(("groups", "nodes"), None, None),
    )
    out_specs = (P("cols", ("groups", "nodes")), P(("groups", "cols"), "nodes"))
    return jax.shard_map(
        on_device, mesh=mesh, in_specs=in_specs, out_specs=out_specs, check_vma=False
    )
```

```python
import functools

import jax
import jax.numpy as jnp
from jax import lax
from jax.experimental import pallas as pl
from jax.experimental.pallas import tpu as pltpu
from jax.sharding import PartitionSpec as P

GRID_X = 32
GRID_Y = 32
PLANE = GRID_X * GRID_Y
LANES = 128
CHUNKS = PLANE // LANES
F32 = jnp.float32
KERNEL_BYTES = 8 * 2**20


def slot_planes():
    odd = lax.rem(lax.axis_index("nodes"), 2)
    return odd, 1 - odd


def split(x):
    high = x.astype(jnp.bfloat16)
    return high, (x - high.astype(F32)).astype(jnp.bfloat16)


def product(left, right, dims):
    left_high, left_low = left
    right_high, right_low = right
    dot = functools.partial(
        lax.dot_general, dimension_numbers=(dims, ((), ())), preferred_element_type=F32
    )
    return dot(left_high, right_high) + (
        dot(left_low, right_high) + dot(left_high, right_low)
    )


def block_product(x, matrix):
    return product(split(x), split(matrix), ((1,), (0,)))


def chunk(k):
    return slice(k * LANES, (k + 1) * LANES)


def plane_chunk(plane, k):
    return pl.ds(pl.multiple_of(plane * PLANE + k * LANES, LANES), LANES)


def lane_index(rows=8):
    return lax.broadcasted_iota(jnp.int32, (rows, LANES), 1)


def ahead_row(here, after):
    lane = lax.broadcasted_iota(jnp.int32, here.shape, here.ndim - 1)
    mixed = here if after is None else jnp.where(lane < GRID_X, after, here)
    return pltpu.roll(mixed, LANES - GRID_X, mixed.ndim - 1)


def behind_row(before, here):
    lane = lax.broadcasted_iota(jnp.int32, here.shape, here.ndim - 1)
    mixed = here if before is None else jnp.where(lane >= LANES - GRID_X, before, here)
    return pltpu.roll(mixed, GRID_X, mixed.ndim - 1)


def plane_springs(couplings, ground, plane, middle, crossing, meets):
    lane = lane_index()
    inside_x = lane % GRID_X < GRID_X - 1

    def row(ref, index, k):
        return jnp.broadcast_to(ref[index : index + 1, plane_chunk(plane, k)], (8, LANES))

    along_y = []
    for k in range(CHUNKS):
        spring = row(couplings, 1, k)
        if k == CHUNKS - 1:
            spring = jnp.where(lane < LANES - GRID_X, spring, 0.0)
        along_y.append(spring)
    result = []
    for k in range(CHUNKS):
        right = jnp.where(inside_x, row(couplings, 0, k), 0.0)
        left = pltpu.roll(right, 1, 1)
        up = along_y[k]
        before = along_y[k - 1] if k else jnp.zeros_like(up)
        down = behind_row(before, up)
        diag = row(ground, 0, k) + (right + left) + (up + down) + (middle[k] + crossing[k])
        halo = jnp.where(meets, crossing[k], 0.0)
        result.append((diag, right, left, up, down, middle[k], halo))
    return result


def all_springs(couplings, ground, got):
    def row_before(slot, k):
        return jnp.broadcast_to(got[slot][0:1, chunk(k)], (8, LANES))

    place, count = lax.axis_index("nodes"), lax.axis_size("nodes")
    odd = lax.rem(place, 2)
    own, mid = [], []
    for k in range(CHUNKS):
        own.append(
            jnp.broadcast_to(
                couplings[2:3, PLANE + k * LANES : PLANE + (k + 1) * LANES], (8, LANES)
            )
        )
        mid.append(jnp.broadcast_to(couplings[2:3, chunk(k)], (8, LANES)))
    result = []
    for slot, plane in enumerate(slot_planes()):
        below = odd == slot
        meets = jnp.where(below, place > 0, place < count - 1)
        crossing = [
            jnp.where(
                below,
                jnp.where(place > 0, row_before(slot, k), 0.0),
                own[k],
            )
            for k in range(CHUNKS)
        ]
        result.append(plane_springs(couplings, ground, plane, mid, crossing, meets))
    return result


def stiff_chunk(springs, k, field, other, halo, rows):
    def load(ref, index):
        return ref[0:rows, chunk(index)].reshape(rows // 8, 8, LANES)

    diag, right, left, up, down, middle, crossing = springs[k]
    here = load(field, k)
    before = load(field, k - 1) if k else None
    after = load(field, k + 1) if k < CHUNKS - 1 else None
    result = diag * here
    result = result - right * pltpu.roll(here, LANES - 1, 2)
    result = result - left * pltpu.roll(here, 1, 2)
    result = result - up * ahead_row(here, after)
    result = result - down * behind_row(before, here)
    result = result - middle * load(other, k)
    result = result - crossing * load(halo, k)
    return result.reshape(rows, LANES)


def first_kernel(forces, precond, out_a, out_b, field, matrices, sems):
    copies = []
    for slot, plane in enumerate(slot_planes()):
        here = pl.ds(pl.multiple_of(plane * PLANE, PLANE), PLANE)
        copies.append(
            (
                pltpu.make_async_copy(forces.at[:, here], field.at[slot], sems.at[slot, 0]),
                pltpu.make_async_copy(
                    precond.at[pl.ds(plane * CHUNKS, CHUNKS)], matrices.at[slot], sems.at[slot, 1]
                ),
            )
        )
    for pair in copies:
        for copy in pair:
            copy.start()
    for slot, out in enumerate((out_a, out_b)):
        for copy in copies[slot]:
            copy.wait()
        for k in range(CHUNKS):
            out[:, chunk(k)] = block_product(field[slot, :, chunk(k)], matrices[slot, k])


def other_kernel(forces, precond, out):
    for slot, plane in enumerate(slot_planes()):
        for k in range(CHUNKS):
            out[slot, :, chunk(k)] = block_product(
                forces[:, plane_chunk(plane, k)], precond[plane * CHUNKS + k]
            )


def second_kernel(couplings, ground, before_a, before_b, precond, d_a, d_b, got_a, got_b, q, w_a, w_b, w_both, near):
    rows = w_a.shape[0]
    springs = all_springs(couplings, ground, (before_a, before_b))
    fields = (d_a, d_b)
    for slot, plane in enumerate(slot_planes()):
        for k in range(CHUNKS):
            image = stiff_chunk(
                springs[slot], k, fields[slot], fields[1 - slot], (got_a, got_b)[slot], rows
            )
            q[slot, :, chunk(k)] = image
            w = block_product(image, precond[plane * CHUNKS + k])
            (w_a, w_b)[slot][:, chunk(k)] = w
            w_both[slot, :, chunk(k)] = w
            near[slot, 0:rows, chunk(k)] = fields[slot][:, chunk(k)]
            near[slot, rows : 2 * rows, chunk(k)] = w


def place_sums(packed, first, sums):
    lane = lane_index(packed.shape[0])
    for index, value in enumerate(sums):
        total = jnp.sum(value, axis=1, keepdims=True)
        packed = jnp.where(lane == first + index, total, packed)
    return packed


def side_kernel(forces, q, near, packed):
    rows = forces.shape[0]
    sums = [jnp.zeros((rows, LANES), F32) for _ in range(3)]
    for slot, plane in enumerate(slot_planes()):
        for k in range(CHUNKS):
            d_here = near[slot, 0:rows, chunk(k)]
            q_here = q[slot, :, chunk(k)]
            sums[0] += forces[:, plane_chunk(plane, k)] * d_here
            sums[1] += d_here * q_here
            sums[2] += q_here * near[slot, rows : 2 * rows, chunk(k)]
    packed[...] = place_sums(jnp.zeros((rows, LANES), F32), 0, sums)


def third_kernel(couplings, ground, before_a, before_b, w_a, w_b, next_a, next_b, packed, v, dots):
    rows = w_a.shape[0]
    springs = all_springs(couplings, ground, (before_a, before_b))
    fields = (w_a, w_b)
    total = jnp.zeros((rows, LANES), F32)
    for slot in range(2):
        for k in range(CHUNKS):
            image = stiff_chunk(
                springs[slot], k, fields[slot], fields[1 - slot], (next_a, next_b)[slot], rows
            )
            v[slot, :, chunk(k)] = image
            total += fields[slot][:, chunk(k)] * image
    values = place_sums(packed[...], 3, [total])
    if rows < LANES:
        values = jnp.concatenate([values, jnp.zeros((LANES - rows, LANES), F32)], axis=0)
    dots[...] = values.T[0:8, :]


def columns_of(fields, slot):
    return jnp.concatenate([field[slot] for field in fields], axis=0)


def early_kernel(n_near, q, v, *refs):
    near, (qv_high, qv_low, near_gram) = refs[:n_near], refs[n_near:]
    sums = [None] * n_near
    for slot in range(2):
        images = split(jnp.concatenate([q[slot], v[slot]], axis=0))
        qv_high[slot], qv_low[slot] = images
        for i in range(n_near):
            term = product(images, split(near[i][slot]), ((1,), (1,)))
            sums[i] = term if slot == 0 else sums[i] + term
    for i in range(n_near):
        near_gram[i] = sums[i]


def far_kernel(qv_high, qv_low, *refs):
    d_far, far_gram = refs[:-1], refs[-1]
    total = None
    for slot in range(2):
        images = (qv_high[slot], qv_low[slot])
        term = product(images, split(columns_of(d_far, slot)), ((1,), (1,)))
        total = term if slot == 0 else total + term
    far_gram[...] = total


def coeffs_kernel(rows, *refs):
    dots, coeffs = refs[:-1], refs[-1]
    total = dots[0][...]
    for piece in dots[1:]:
        total = total + piece[...]
    rz0, dq, qw, wv = (total[i : i + 1, :] for i in range(4))
    alpha0 = rz0 / dq
    rz1 = alpha0 * alpha0 * qw - rz0
    grow = 1.0 + rz1 / rz0
    curve1 = grow * grow * dq - 2.0 * alpha0 * grow * qw + alpha0 * alpha0 * wv
    alpha1 = rz1 / curve1
    used = lane_index(1) < rows
    on_d = jnp.where(used, alpha0 + alpha1 * grow, 0.0)
    on_w = jnp.where(used, -alpha0 * alpha1, 0.0)
    pair = jnp.concatenate([on_d, on_w, jnp.zeros((6, LANES), F32)], axis=0)
    for i in range(coeffs.shape[0] // 8):
        coeffs[8 * i : 8 * i + 8, :] = pair


def late_kernel(n_near, n_far, exchange, coeffs, qv_high, qv_low, near_gram, far_gram, *refs):
    far, outs, gram = refs[:n_far], refs[n_far:-1], refs[-1]
    rows = near_gram.shape[1] // 2
    far_sum = None
    for slot in range(2):
        images = (qv_high[slot], qv_low[slot])
        term = product(images, split(columns_of(far, slot)), ((1,), (1,)))
        far_sum = term if slot == 0 else far_sum + term
    p, s = turned(coeffs, rows)
    if not exchange:
        gram = outs[0]
    for i in range(n_near):
        gram[i] = p * near_gram[i, 0:rows] + s * near_gram[i, rows : 2 * rows]
    d_part = far_gram[...]
    for i in range(n_far):
        there = slice(i * rows, (i + 1) * rows)
        both = jnp.concatenate([d_part[:, there], far_sum[:, there]], axis=1)
        gram[n_near + i] = p * both[0:rows] + s * both[rows : 2 * rows]
    if exchange:
        mine = lax.axis_index("nodes") ^ lax.axis_index("cols")
        for i in range(n_near + n_far):
            outs[i][...] = gram[mine ^ i]


def turned(coeffs, rows):
    table = jnp.concatenate([coeffs[0:8, :], jnp.zeros((LANES - 8, LANES), F32)], axis=0).T
    return [jnp.broadcast_to(table[0:rows, i : i + 1], (rows, LANES)) for i in range(2)]


def modes_kernel(coeffs, near, modes):
    rows = modes.shape[0]
    p, s = turned(coeffs, rows)
    for slot, plane in enumerate(slot_planes()):
        for k in range(CHUNKS):
            modes[:, plane_chunk(plane, k)] = (
                p * near[slot, 0:rows, chunk(k)] + s * near[slot, rows : 2 * rows, chunk(k)]
            )


def fifth_kernel(scale, n_sums, *refs):
    sums, coeffs_of, tile = refs[:n_sums], refs[n_sums:-1], refs[-1]
    rows = tile.shape[0]
    total = sums[0][...]
    for piece in sums[1:]:
        total = total + piece[...]
    mine = lax.axis_index("nodes") ^ lax.axis_index("cols")
    coeffs = coeffs_of[0][0:8, :]
    for i in range(1, n_sums):
        coeffs = jnp.where(mine == i, coeffs_of[i][0:8, :], coeffs)
    tile[...] = (
        coeffs[0:1, 0:rows] * total[:, 0:rows] + coeffs[1:2, 0:rows] * total[:, rows : 2 * rows]
    ) * scale


def call(kernel, name, args, shapes, scratch=(), space=pltpu.VMEM):
    shapes = [
        shape if isinstance(shape, jax.ShapeDtypeStruct) else jax.ShapeDtypeStruct(shape, F32)
        for shape in shapes
    ]
    return pl.pallas_call(
        kernel,
        out_shape=shapes,
        in_specs=[pl.BlockSpec(memory_space=space)] * len(args),
        out_specs=[pl.BlockSpec(memory_space=pltpu.VMEM)] * len(shapes),
        scratch_shapes=scratch,
        compiler_params=pltpu.CompilerParams(vmem_limit_bytes=KERNEL_BYTES),
        name=name,
    )(*args)


def neighbours(block, first):
    nodes, cols = lax.axis_size("nodes"), lax.axis_size("cols")
    route = []
    for n in range(nodes):
        other = n + 1 if n % 2 == first else n - 1
        for c in range(cols):
            here = n * cols + c
            if 0 <= other < nodes:
                route.append((here, other * cols + c))
            elif cols % 2 == 0:
                route.append((here, here ^ 1))
    return lax.ppermute(block, ("nodes", "cols"), route)


def swapped(block, axis, bit):
    return lax.ppermute(block, axis, [(i, i ^ bit) for i in range(lax.axis_size(axis))])


def on_device(forces, couplings, ground, precond):
    rows, length = forces.shape
    nodes, cols = lax.axis_size("nodes"), lax.axis_size("cols")
    ground = ground.reshape(1, length)
    bits = []
    while 2 ** len(bits) < cols:
        bits.append(2 ** len(bits))
    top = cols // 2

    def shared(block):
        held = {0: block}
        for bit in bits[:-1]:
            for key in list(held):
                held[key ^ bit] = swapped(held[key], "cols", bit)
        return [held[key] for key in range(max(top, 1))]

    field = (rows, PLANE)
    d_a, d_b = call(
        first_kernel,
        "first",
        [pltpu.with_memory_space_constraint(x, pltpu.HBM) for x in (forces, precond)],
        [field] * 2,
        [
            pltpu.VMEM((2, rows, PLANE), F32),
            pltpu.VMEM((2, CHUNKS, LANES, LANES), F32),
            pltpu.SemaphoreType.DMA((2, 2)),
        ],
        pltpu.HBM,
    )
    got_a, got_b = neighbours(d_a, 1), neighbours(d_b, 0)
    forces_far = swapped(forces, "cols", top)
    last = couplings[2:3, length - PLANE :]
    before_a, before_b = neighbours(last, 1), neighbours(last, 0)
    got_a, got_b, forces_far = lax.optimization_barrier((got_a, got_b, forces_far))
    edges = (couplings, ground, before_a, before_b)
    q, w_a, w_b, w_both, near = call(
        second_kernel,
        "second",
        (*edges, precond, d_a, d_b, got_a, got_b),
        [(2,) + field, field, field, (2,) + field, (2, 2 * rows, PLANE)],
    )
    next_a, next_b = neighbours(w_a, 1), neighbours(w_b, 0)
    far = swapped(w_both, "cols", top)
    near = shared(near)
    (d_far,) = call(other_kernel, "other", (forces_far, precond), [(2,) + field])
    next_a, next_b, d_far, near = lax.optimization_barrier((next_a, next_b, d_far, near))
    d_far = shared(d_far)
    (packed,) = call(side_kernel, "side", (forces, q, near[0]), [(rows, LANES)])
    v, dots = call(
        third_kernel,
        "third",
        (*edges, w_a, w_b, next_a, next_b, packed),
        [(2,) + field, (8, LANES)],
    )
    exchange = nodes == cols
    if exchange:
        dots = [dots] + [swapped(dots, "nodes", i) for i in range(1, nodes)]
    else:
        dots = [lax.psum(dots, "nodes")]
    halves = jax.ShapeDtypeStruct((2, 2 * rows, PLANE), jnp.bfloat16)
    qv_high, qv_low, near_gram = call(
        functools.partial(early_kernel, len(near)),
        "early",
        (q, v, *near),
        [halves, halves, (len(near), 2 * rows, 2 * rows)],
    )
    d_far, far = lax.optimization_barrier((d_far, far))
    (far_gram,) = call(
        far_kernel, "far", (qv_high, qv_low, *d_far), [(2 * rows, len(d_far) * rows)]
    )
    far, far_gram, *dots = lax.optimization_barrier((far, far_gram, *dots))
    far = shared(far)
    (coeffs,) = call(functools.partial(coeffs_kernel, rows), "coeffs", dots, [(rows + 8, LANES)])
    grams = call(
        functools.partial(late_kernel, len(near), len(d_far), exchange),
        "late",
        (coeffs, qv_high, qv_low, near_gram, far_gram, *far),
        [(rows, LANES)] * cols if exchange else [(cols, rows, LANES)],
        [pltpu.VMEM((cols, rows, LANES), F32)],
    )
    scale = 1.0 / (length * nodes)
    (modes,) = call(modes_kernel, "modes", (coeffs, near[0]), [(rows, length)])
    if exchange:
        theirs = [coeffs] + [swapped(coeffs, "cols", i) for i in range(1, cols)]
        sums = [grams[0]] + [swapped(grams[i], "nodes", i) for i in reversed(range(1, nodes))]
        (tile,) = call(
            functools.partial(fifth_kernel, scale, nodes),
            "fifth",
            (*sums, *theirs),
            [(rows, rows)],
        )
    else:
        gram = grams[0]
        every = lax.all_gather(coeffs, "cols")
        mine = lax.axis_index("cols")
        parts = []
        for i in range(cols):
            block = lax.dynamic_index_in_dim(gram, mine ^ i, 0, keepdims=False)
            parts.append(
                every[i, 0:1, 0:rows] * block[:, 0:rows]
                + every[i, 1:2, 0:rows] * block[:, rows : 2 * rows]
            )
        partial = jnp.concatenate(parts, axis=1) * scale
        tile = lax.psum_scatter(partial, "nodes", scatter_dimension=1, tiled=True)
    return (modes, tile)


def solution(mesh):
    in_specs = (
        P("cols", ("groups", "nodes")),
        P(None, ("groups", "nodes")),
        P(("groups", "nodes")),
        P(("groups", "nodes"), None, None),
    )
    out_specs = (P("cols", ("groups", "nodes")), P(("groups", "cols"), "nodes"))
    return jax.shard_map(
        on_device, mesh=mesh, in_specs=in_specs, out_specs=out_specs, check_vma=False
    )
```

```python
import functools

import jax
import jax.numpy as jnp
from jax import lax
from jax.experimental import pallas as pl
from jax.experimental.pallas import tpu as pltpu
from jax.sharding import PartitionSpec as P

GRID_X = 32
GRID_Y = 32
PLANE = GRID_X * GRID_Y
LANES = 128
CHUNKS = PLANE // LANES
F32 = jnp.float32
KERNEL_BYTES = 8 * 2**20


def slot_planes():
    odd = lax.rem(lax.axis_index("nodes"), 2)
    return odd, 1 - odd


def split(x):
    high = x.astype(jnp.bfloat16)
    return high, (x - high.astype(F32)).astype(jnp.bfloat16)


def product(left, right, dims):
    left_high, left_low = left
    right_high, right_low = right
    dot = functools.partial(
        lax.dot_general, dimension_numbers=(dims, ((), ())), preferred_element_type=F32
    )
    return dot(left_high, right_high) + (
        dot(left_low, right_high) + dot(left_high, right_low)
    )


def block_product(x, matrix):
    return product(split(x), split(matrix), ((1,), (0,)))


def chunk(k):
    return slice(k * LANES, (k + 1) * LANES)


def plane_chunk(plane, k):
    return pl.ds(pl.multiple_of(plane * PLANE + k * LANES, LANES), LANES)


def lane_index(rows=8):
    return lax.broadcasted_iota(jnp.int32, (rows, LANES), 1)


def ahead_row(here, after):
    lane = lax.broadcasted_iota(jnp.int32, here.shape, here.ndim - 1)
    mixed = here if after is None else jnp.where(lane < GRID_X, after, here)
    return pltpu.roll(mixed, LANES - GRID_X, mixed.ndim - 1)


def behind_row(before, here):
    lane = lax.broadcasted_iota(jnp.int32, here.shape, here.ndim - 1)
    mixed = here if before is None else jnp.where(lane >= LANES - GRID_X, before, here)
    return pltpu.roll(mixed, GRID_X, mixed.ndim - 1)


def plane_springs(couplings, ground, plane, middle, crossing, meets):
    lane = lane_index()
    inside_x = lane % GRID_X < GRID_X - 1

    def row(ref, index, k):
        return jnp.broadcast_to(ref[index : index + 1, plane_chunk(plane, k)], (8, LANES))

    along_y = []
    for k in range(CHUNKS):
        spring = row(couplings, 1, k)
        if k == CHUNKS - 1:
            spring = jnp.where(lane < LANES - GRID_X, spring, 0.0)
        along_y.append(spring)
    result = []
    for k in range(CHUNKS):
        right = jnp.where(inside_x, row(couplings, 0, k), 0.0)
        left = pltpu.roll(right, 1, 1)
        up = along_y[k]
        before = along_y[k - 1] if k else jnp.zeros_like(up)
        down = behind_row(before, up)
        diag = row(ground, 0, k) + (right + left) + (up + down) + (middle[k] + crossing[k])
        halo = jnp.where(meets, crossing[k], 0.0)
        result.append((diag, right, left, up, down, middle[k], halo))
    return result


def all_springs(couplings, ground, got):
    def row_before(slot, k):
        return jnp.broadcast_to(got[slot][0:1, chunk(k)], (8, LANES))

    place, count = lax.axis_index("nodes"), lax.axis_size("nodes")
    odd = lax.rem(place, 2)
    own, mid = [], []
    for k in range(CHUNKS):
        own.append(
            jnp.broadcast_to(
                couplings[2:3, PLANE + k * LANES : PLANE + (k + 1) * LANES], (8, LANES)
            )
        )
        mid.append(jnp.broadcast_to(couplings[2:3, chunk(k)], (8, LANES)))
    result = []
    for slot, plane in enumerate(slot_planes()):
        below = odd == slot
        meets = jnp.where(below, place > 0, place < count - 1)
        crossing = [
            jnp.where(
                below,
                jnp.where(place > 0, row_before(slot, k), 0.0),
                own[k],
            )
            for k in range(CHUNKS)
        ]
        result.append(plane_springs(couplings, ground, plane, mid, crossing, meets))
    return result


def stiff_chunk(springs, k, field, other, halo, rows):
    def load(ref, index):
        return ref[0:rows, chunk(index)].reshape(rows // 8, 8, LANES)

    diag, right, left, up, down, middle, crossing = springs[k]
    here = load(field, k)
    before = load(field, k - 1) if k else None
    after = load(field, k + 1) if k < CHUNKS - 1 else None
    result = diag * here
    result = result - right * pltpu.roll(here, LANES - 1, 2)
    result = result - left * pltpu.roll(here, 1, 2)
    result = result - up * ahead_row(here, after)
    result = result - down * behind_row(before, here)
    result = result - middle * load(other, k)
    result = result - crossing * load(halo, k)
    return result.reshape(rows, LANES)


def first_kernel(forces, precond, out_a, out_b, field, matrices, sems):
    copies = []
    for slot, plane in enumerate(slot_planes()):
        here = pl.ds(pl.multiple_of(plane * PLANE, PLANE), PLANE)
        copies.append(
            (
                pltpu.make_async_copy(forces.at[:, here], field.at[slot], sems.at[slot, 0]),
                pltpu.make_async_copy(
                    precond.at[pl.ds(plane * CHUNKS, CHUNKS)], matrices.at[slot], sems.at[slot, 1]
                ),
            )
        )
    for pair in copies:
        for copy in pair:
            copy.start()
    for slot, out in enumerate((out_a, out_b)):
        for copy in copies[slot]:
            copy.wait()
        for k in range(CHUNKS):
            out[:, chunk(k)] = block_product(field[slot, :, chunk(k)], matrices[slot, k])


def place_sums(packed, first, sums):
    lane = lane_index(packed.shape[0])
    for index, value in enumerate(sums):
        total = jnp.sum(value, axis=1, keepdims=True)
        packed = jnp.where(lane == first + index, total, packed)
    return packed


def other_kernel(forces_far, precond, forces, q, near, d_far, packed):
    rows = forces.shape[0]
    sums = [jnp.zeros((rows, LANES), F32) for _ in range(3)]
    for slot, plane in enumerate(slot_planes()):
        for k in range(CHUNKS):
            d_far[slot, :, chunk(k)] = block_product(
                forces_far[:, plane_chunk(plane, k)], precond[plane * CHUNKS + k]
            )
            d_here = near[slot, 0:rows, chunk(k)]
            q_here = q[slot, :, chunk(k)]
            sums[0] += forces[:, plane_chunk(plane, k)] * d_here
            sums[1] += d_here * q_here
            sums[2] += q_here * near[slot, rows : 2 * rows, chunk(k)]
    packed[...] = place_sums(jnp.zeros((rows, LANES), F32), 0, sums)


def second_kernel(couplings, ground, before_a, before_b, precond, d_a, d_b, got_a, got_b, q, w_a, w_b, w_both, near):
    rows = w_a.shape[0]
    springs = all_springs(couplings, ground, (before_a, before_b))
    fields = (d_a, d_b)
    for slot, plane in enumerate(slot_planes()):
        for k in range(CHUNKS):
            image = stiff_chunk(
                springs[slot], k, fields[slot], fields[1 - slot], (got_a, got_b)[slot], rows
            )
            q[slot, :, chunk(k)] = image
            w = block_product(image, precond[plane * CHUNKS + k])
            (w_a, w_b)[slot][:, chunk(k)] = w
            w_both[slot, :, chunk(k)] = w
            near[slot, 0:rows, chunk(k)] = fields[slot][:, chunk(k)]
            near[slot, rows : 2 * rows, chunk(k)] = w


def third_kernel(couplings, ground, before_a, before_b, w_a, w_b, next_a, next_b, packed, v, dots):
    rows = w_a.shape[0]
    springs = all_springs(couplings, ground, (before_a, before_b))
    fields = (w_a, w_b)
    total = jnp.zeros((rows, LANES), F32)
    for slot in range(2):
        for k in range(CHUNKS):
            image = stiff_chunk(
                springs[slot], k, fields[slot], fields[1 - slot], (next_a, next_b)[slot], rows
            )
            v[slot, :, chunk(k)] = image
            total += fields[slot][:, chunk(k)] * image
    values = place_sums(packed[...], 3, [total])
    if rows < LANES:
        values = jnp.concatenate([values, jnp.zeros((LANES - rows, LANES), F32)], axis=0)
    dots[...] = values.T[0:8, :]


def columns_of(fields, slot):
    return jnp.concatenate([field[slot] for field in fields], axis=0)


def early_kernel(n_near, q, v, *refs):
    near, (qv_high, qv_low, near_gram) = refs[:n_near], refs[n_near:]
    sums = [None] * n_near
    for slot in range(2):
        images = split(jnp.concatenate([q[slot], v[slot]], axis=0))
        qv_high[slot], qv_low[slot] = images
        for i in range(n_near):
            term = product(images, split(near[i][slot]), ((1,), (1,)))
            sums[i] = term if slot == 0 else sums[i] + term
    for i in range(n_near):
        near_gram[i] = sums[i]


def far_kernel(qv_high, qv_low, *refs):
    d_far, far_gram = refs[:-1], refs[-1]
    total = None
    for slot in range(2):
        images = (qv_high[slot], qv_low[slot])
        term = product(images, split(columns_of(d_far, slot)), ((1,), (1,)))
        total = term if slot == 0 else total + term
    far_gram[...] = total


def coeffs_kernel(rows, *refs):
    dots, coeffs = refs[:-1], refs[-1]
    total = dots[0][...]
    for piece in dots[1:]:
        total = total + piece[...]
    rz0, dq, qw, wv = (total[i : i + 1, :] for i in range(4))
    alpha0 = rz0 / dq
    rz1 = alpha0 * alpha0 * qw - rz0
    grow = 1.0 + rz1 / rz0
    curve1 = grow * grow * dq - 2.0 * alpha0 * grow * qw + alpha0 * alpha0 * wv
    alpha1 = rz1 / curve1
    used = lane_index(1) < rows
    on_d = jnp.where(used, alpha0 + alpha1 * grow, 0.0)
    on_w = jnp.where(used, -alpha0 * alpha1, 0.0)
    pair = jnp.concatenate([on_d, on_w, jnp.zeros((6, LANES), F32)], axis=0)
    for i in range(coeffs.shape[0] // 8):
        coeffs[8 * i : 8 * i + 8, :] = pair


def late_kernel(n_near, n_far, exchange, coeffs, qv_high, qv_low, near_gram, far_gram, *refs):
    far, outs, gram = refs[:n_far], refs[n_far:-1], refs[-1]
    rows = near_gram.shape[1] // 2
    far_sum = None
    for slot in range(2):
        images = (qv_high[slot], qv_low[slot])
        term = product(images, split(columns_of(far, slot)), ((1,), (1,)))
        far_sum = term if slot == 0 else far_sum + term
    p, s = turned(coeffs, rows)
    if not exchange:
        gram = outs[0]
    for i in range(n_near):
        gram[i] = p * near_gram[i, 0:rows] + s * near_gram[i, rows : 2 * rows]
    d_part = far_gram[...]
    for i in range(n_far):
        there = slice(i * rows, (i + 1) * rows)
        both = jnp.concatenate([d_part[:, there], far_sum[:, there]], axis=1)
        gram[n_near + i] = p * both[0:rows] + s * both[rows : 2 * rows]
    if exchange:
        mine = lax.axis_index("nodes") ^ lax.axis_index("cols")
        for i in range(n_near + n_far):
            outs[i][...] = gram[mine ^ i]


def turned(coeffs, rows):
    table = jnp.concatenate([coeffs[0:8, :], jnp.zeros((LANES - 8, LANES), F32)], axis=0).T
    return [jnp.broadcast_to(table[0:rows, i : i + 1], (rows, LANES)) for i in range(2)]


def modes_kernel(coeffs, near, modes):
    rows = modes.shape[0]
    p, s = turned(coeffs, rows)
    for slot, plane in enumerate(slot_planes()):
        for k in range(CHUNKS):
            modes[:, plane_chunk(plane, k)] = (
                p * near[slot, 0:rows, chunk(k)] + s * near[slot, rows : 2 * rows, chunk(k)]
            )


def fifth_kernel(scale, n_sums, *refs):
    sums, coeffs_of, tile = refs[:n_sums], refs[n_sums:-1], refs[-1]
    rows = tile.shape[0]
    total = sums[0][...]
    for piece in sums[1:]:
        total = total + piece[...]
    mine = lax.axis_index("nodes") ^ lax.axis_index("cols")
    coeffs = coeffs_of[0][0:8, :]
    for i in range(1, n_sums):
        coeffs = jnp.where(mine == i, coeffs_of[i][0:8, :], coeffs)
    tile[...] = (
        coeffs[0:1, 0:rows] * total[:, 0:rows] + coeffs[1:2, 0:rows] * total[:, rows : 2 * rows]
    ) * scale


def call(kernel, name, args, shapes, scratch=(), space=pltpu.VMEM):
    shapes = [
        shape if isinstance(shape, jax.ShapeDtypeStruct) else jax.ShapeDtypeStruct(shape, F32)
        for shape in shapes
    ]
    return pl.pallas_call(
        kernel,
        out_shape=shapes,
        in_specs=[pl.BlockSpec(memory_space=space)] * len(args),
        out_specs=[pl.BlockSpec(memory_space=pltpu.VMEM)] * len(shapes),
        scratch_shapes=scratch,
        compiler_params=pltpu.CompilerParams(vmem_limit_bytes=KERNEL_BYTES),
        name=name,
    )(*args)


def neighbours(block, first):
    nodes, cols = lax.axis_size("nodes"), lax.axis_size("cols")
    route = []
    for n in range(nodes):
        other = n + 1 if n % 2 == first else n - 1
        for c in range(cols):
            here = n * cols + c
            if 0 <= other < nodes:
                route.append((here, other * cols + c))
            elif cols % 2 == 0:
                route.append((here, here ^ 1))
    return lax.ppermute(block, ("nodes", "cols"), route)


def swapped(block, axis, bit):
    return lax.ppermute(block, axis, [(i, i ^ bit) for i in range(lax.axis_size(axis))])


def on_device(forces, couplings, ground, precond):
    rows, length = forces.shape
    nodes, cols = lax.axis_size("nodes"), lax.axis_size("cols")
    ground = ground.reshape(1, length)
    bits = []
    while 2 ** len(bits) < cols:
        bits.append(2 ** len(bits))
    top = cols // 2

    def shared(block):
        held = {0: block}
        for bit in bits[:-1]:
            for key in list(held):
                held[key ^ bit] = swapped(held[key], "cols", bit)
        return [held[key] for key in range(max(top, 1))]

    field = (rows, PLANE)
    d_a, d_b = call(
        first_kernel,
        "first",
        [pltpu.with_memory_space_constraint(x, pltpu.HBM) for x in (forces, precond)],
        [field] * 2,
        [
            pltpu.VMEM((2, rows, PLANE), F32),
            pltpu.VMEM((2, CHUNKS, LANES, LANES), F32),
            pltpu.SemaphoreType.DMA((2, 2)),
        ],
        pltpu.HBM,
    )
    got_a, got_b = neighbours(d_a, 1), neighbours(d_b, 0)
    forces_far = swapped(forces, "cols", top)
    last = couplings[2:3, length - PLANE :]
    before_a, before_b = neighbours(last, 1), neighbours(last, 0)
    got_a, got_b, forces_far = lax.optimization_barrier((got_a, got_b, forces_far))
    edges = (couplings, ground, before_a, before_b)
    q, w_a, w_b, w_both, near = call(
        second_kernel,
        "second",
        (*edges, precond, d_a, d_b, got_a, got_b),
        [(2,) + field, field, field, (2,) + field, (2, 2 * rows, PLANE)],
    )
    next_a, next_b = neighbours(w_a, 1), neighbours(w_b, 0)
    far = swapped(w_both, "cols", top)
    near = shared(near)
    d_far, packed = call(
        other_kernel,
        "other",
        (forces_far, precond, forces, q, near[0]),
        [(2,) + field, (rows, LANES)],
    )
    next_a, next_b, d_far, near = lax.optimization_barrier((next_a, next_b, d_far, near))
    d_far = shared(d_far)
    v, dots = call(
        third_kernel,
        "third",
        (*edges, w_a, w_b, next_a, next_b, packed),
        [(2,) + field, (8, LANES)],
    )
    exchange = nodes == cols
    if exchange:
        dots = [dots] + [swapped(dots, "nodes", i) for i in range(1, nodes)]
    else:
        dots = [lax.psum(dots, "nodes")]
    halves = jax.ShapeDtypeStruct((2, 2 * rows, PLANE), jnp.bfloat16)
    qv_high, qv_low, near_gram = call(
        functools.partial(early_kernel, len(near)),
        "early",
        (q, v, *near),
        [halves, halves, (len(near), 2 * rows, 2 * rows)],
    )
    d_far, far = lax.optimization_barrier((d_far, far))
    (far_gram,) = call(
        far_kernel, "far", (qv_high, qv_low, *d_far), [(2 * rows, len(d_far) * rows)]
    )
    far, far_gram, *dots = lax.optimization_barrier((far, far_gram, *dots))
    far = shared(far)
    (coeffs,) = call(functools.partial(coeffs_kernel, rows), "coeffs", dots, [(rows + 8, LANES)])
    grams = call(
        functools.partial(late_kernel, len(near), len(d_far), exchange),
        "late",
        (coeffs, qv_high, qv_low, near_gram, far_gram, *far),
        [(rows, LANES)] * cols if exchange else [(cols, rows, LANES)],
        [pltpu.VMEM((cols, rows, LANES), F32)],
    )
    scale = 1.0 / (length * nodes)
    (modes,) = call(modes_kernel, "modes", (coeffs, near[0]), [(rows, length)])
    if exchange:
        theirs = [coeffs] + [swapped(coeffs, "cols", i) for i in range(1, cols)]
        sums = [grams[0]] + [swapped(grams[i], "nodes", i) for i in reversed(range(1, nodes))]
        (tile,) = call(
            functools.partial(fifth_kernel, scale, nodes),
            "fifth",
            (*sums, *theirs),
            [(rows, rows)],
        )
    else:
        gram = grams[0]
        every = lax.all_gather(coeffs, "cols")
        mine = lax.axis_index("cols")
        parts = []
        for i in range(cols):
            block = lax.dynamic_index_in_dim(gram, mine ^ i, 0, keepdims=False)
            parts.append(
                every[i, 0:1, 0:rows] * block[:, 0:rows]
                + every[i, 1:2, 0:rows] * block[:, rows : 2 * rows]
            )
        partial = jnp.concatenate(parts, axis=1) * scale
        tile = lax.psum_scatter(partial, "nodes", scatter_dimension=1, tiled=True)
    return (modes, tile)


def solution(mesh):
    in_specs = (
        P("cols", ("groups", "nodes")),
        P(None, ("groups", "nodes")),
        P(("groups", "nodes")),
        P(("groups", "nodes"), None, None),
    )
    out_specs = (P("cols", ("groups", "nodes")), P(("groups", "cols"), "nodes"))
    return jax.shard_map(
        on_device, mesh=mesh, in_specs=in_specs, out_specs=out_specs, check_vma=False
    )
```

```python
import functools

import jax
import jax.numpy as jnp
from jax import lax
from jax.experimental import pallas as pl
from jax.experimental.pallas import tpu as pltpu
from jax.sharding import PartitionSpec as P

GRID_X = 32
GRID_Y = 32
PLANE = GRID_X * GRID_Y
LANES = 128
CHUNKS = PLANE // LANES
F32 = jnp.float32
KERNEL_BYTES = 8 * 2**20


def slot_planes():
    odd = lax.rem(lax.axis_index("nodes"), 2)
    return odd, 1 - odd


def split(x):
    high = x.astype(jnp.bfloat16)
    return high, (x - high.astype(F32)).astype(jnp.bfloat16)


def product(left, right, dims):
    left_high, left_low = left
    right_high, right_low = right
    dot = functools.partial(
        lax.dot_general, dimension_numbers=(dims, ((), ())), preferred_element_type=F32
    )
    return dot(left_high, right_high) + (
        dot(left_low, right_high) + dot(left_high, right_low)
    )


def block_product(x, matrix):
    return product(split(x), split(matrix), ((1,), (0,)))


def chunk(k):
    return slice(k * LANES, (k + 1) * LANES)


def plane_chunk(plane, k):
    return pl.ds(pl.multiple_of(plane * PLANE + k * LANES, LANES), LANES)


def lane_index(rows=8):
    return lax.broadcasted_iota(jnp.int32, (rows, LANES), 1)


def ahead_row(here, after):
    lane = lax.broadcasted_iota(jnp.int32, here.shape, here.ndim - 1)
    mixed = here if after is None else jnp.where(lane < GRID_X, after, here)
    return pltpu.roll(mixed, LANES - GRID_X, mixed.ndim - 1)


def behind_row(before, here):
    lane = lax.broadcasted_iota(jnp.int32, here.shape, here.ndim - 1)
    mixed = here if before is None else jnp.where(lane >= LANES - GRID_X, before, here)
    return pltpu.roll(mixed, GRID_X, mixed.ndim - 1)


def plane_springs(couplings, ground, plane, middle, crossing, meets):
    lane = lane_index()
    inside_x = lane % GRID_X < GRID_X - 1

    def row(ref, index, k):
        return jnp.broadcast_to(ref[index : index + 1, plane_chunk(plane, k)], (8, LANES))

    along_y = []
    for k in range(CHUNKS):
        spring = row(couplings, 1, k)
        if k == CHUNKS - 1:
            spring = jnp.where(lane < LANES - GRID_X, spring, 0.0)
        along_y.append(spring)
    result = []
    for k in range(CHUNKS):
        right = jnp.where(inside_x, row(couplings, 0, k), 0.0)
        left = pltpu.roll(right, 1, 1)
        up = along_y[k]
        before = along_y[k - 1] if k else jnp.zeros_like(up)
        down = behind_row(before, up)
        diag = row(ground, 0, k) + (right + left) + (up + down) + (middle[k] + crossing[k])
        halo = jnp.where(meets, crossing[k], 0.0)
        result.append((diag, right, left, up, down, middle[k], halo))
    return result


def all_springs(couplings, ground, got):
    def row_before(slot, k):
        return jnp.broadcast_to(got[slot][0:1, chunk(k)], (8, LANES))

    place, count = lax.axis_index("nodes"), lax.axis_size("nodes")
    odd = lax.rem(place, 2)
    own, mid = [], []
    for k in range(CHUNKS):
        own.append(
            jnp.broadcast_to(
                couplings[2:3, PLANE + k * LANES : PLANE + (k + 1) * LANES], (8, LANES)
            )
        )
        mid.append(jnp.broadcast_to(couplings[2:3, chunk(k)], (8, LANES)))
    result = []
    for slot, plane in enumerate(slot_planes()):
        below = odd == slot
        meets = jnp.where(below, place > 0, place < count - 1)
        crossing = [
            jnp.where(
                below,
                jnp.where(place > 0, row_before(slot, k), 0.0),
                own[k],
            )
            for k in range(CHUNKS)
        ]
        result.append(plane_springs(couplings, ground, plane, mid, crossing, meets))
    return result


def stiff_chunk(springs, k, field, other, halo, rows):
    def load(ref, index):
        return ref[0:rows, chunk(index)].reshape(rows // 8, 8, LANES)

    diag, right, left, up, down, middle, crossing = springs[k]
    here = load(field, k)
    before = load(field, k - 1) if k else None
    after = load(field, k + 1) if k < CHUNKS - 1 else None
    result = diag * here
    result = result - right * pltpu.roll(here, LANES - 1, 2)
    result = result - left * pltpu.roll(here, 1, 2)
    result = result - up * ahead_row(here, after)
    result = result - down * behind_row(before, here)
    result = result - middle * load(other, k)
    result = result - crossing * load(halo, k)
    return result.reshape(rows, LANES)


def first_kernel(forces, precond, out_a, out_b, field, matrices, sems):
    copies = []
    for slot, plane in enumerate(slot_planes()):
        here = pl.ds(pl.multiple_of(plane * PLANE, PLANE), PLANE)
        copies.append(
            (
                pltpu.make_async_copy(forces.at[:, here], field.at[slot], sems.at[slot, 0]),
                pltpu.make_async_copy(
                    precond.at[pl.ds(plane * CHUNKS, CHUNKS)], matrices.at[slot], sems.at[slot, 1]
                ),
            )
        )
    for pair in copies:
        for copy in pair:
            copy.start()
    for slot, out in enumerate((out_a, out_b)):
        for copy in copies[slot]:
            copy.wait()
        for k in range(CHUNKS):
            out[:, chunk(k)] = block_product(field[slot, :, chunk(k)], matrices[slot, k])


def place_sums(packed, first, sums):
    lane = lane_index(packed.shape[0])
    for index, value in enumerate(sums):
        total = jnp.sum(value, axis=1, keepdims=True)
        packed = jnp.where(lane == first + index, total, packed)
    return packed


def other_kernel(forces_far, precond, forces, q, near, d_far, packed):
    rows = forces.shape[0]
    sums = [jnp.zeros((rows, LANES), F32) for _ in range(3)]
    for slot, plane in enumerate(slot_planes()):
        for k in range(CHUNKS):
            d_far[slot, :, chunk(k)] = block_product(
                forces_far[:, plane_chunk(plane, k)], precond[plane * CHUNKS + k]
            )
            d_here = near[slot, 0:rows, chunk(k)]
            q_here = q[slot, :, chunk(k)]
            sums[0] += forces[:, plane_chunk(plane, k)] * d_here
            sums[1] += d_here * q_here
            sums[2] += q_here * near[slot, rows : 2 * rows, chunk(k)]
    packed[...] = place_sums(jnp.zeros((rows, LANES), F32), 0, sums)


def second_kernel(couplings, ground, before_a, before_b, precond, d_a, d_b, got_a, got_b, q, w_a, w_b, w_both, near):
    rows = w_a.shape[0]
    springs = all_springs(couplings, ground, (before_a, before_b))
    fields = (d_a, d_b)
    for slot, plane in enumerate(slot_planes()):
        for k in range(CHUNKS):
            image = stiff_chunk(
                springs[slot], k, fields[slot], fields[1 - slot], (got_a, got_b)[slot], rows
            )
            q[slot, :, chunk(k)] = image
            w = block_product(image, precond[plane * CHUNKS + k])
            (w_a, w_b)[slot][:, chunk(k)] = w
            w_both[slot, :, chunk(k)] = w
            near[slot, 0:rows, chunk(k)] = fields[slot][:, chunk(k)]
            near[slot, rows : 2 * rows, chunk(k)] = w


def third_kernel(couplings, ground, before_a, before_b, w_a, w_b, next_a, next_b, packed, v, dots):
    rows = w_a.shape[0]
    springs = all_springs(couplings, ground, (before_a, before_b))
    fields = (w_a, w_b)
    total = jnp.zeros((rows, LANES), F32)
    for slot in range(2):
        for k in range(CHUNKS):
            image = stiff_chunk(
                springs[slot], k, fields[slot], fields[1 - slot], (next_a, next_b)[slot], rows
            )
            v[slot, :, chunk(k)] = image
            total += fields[slot][:, chunk(k)] * image
    values = place_sums(packed[...], 3, [total])
    if rows < LANES:
        values = jnp.concatenate([values, jnp.zeros((LANES - rows, LANES), F32)], axis=0)
    dots[...] = values.T[0:8, :]


def columns_of(fields, slot):
    return jnp.concatenate([field[slot] for field in fields], axis=0)


def early_kernel(n_near, q, v, *refs):
    near, (qv_high, qv_low, near_gram) = refs[:n_near], refs[n_near:]
    sums = [None] * n_near
    for slot in range(2):
        images = split(jnp.concatenate([q[slot], v[slot]], axis=0))
        qv_high[slot], qv_low[slot] = images
        for i in range(n_near):
            term = product(images, split(near[i][slot]), ((1,), (1,)))
            sums[i] = term if slot == 0 else sums[i] + term
    for i in range(n_near):
        near_gram[i] = sums[i]


def far_kernel(qv_high, qv_low, *refs):
    d_far, far_gram = refs[:-1], refs[-1]
    total = None
    for slot in range(2):
        images = (qv_high[slot], qv_low[slot])
        term = product(images, split(columns_of(d_far, slot)), ((1,), (1,)))
        total = term if slot == 0 else total + term
    far_gram[...] = total


def coeffs_kernel(rows, *refs):
    dots, coeffs = refs[:-1], refs[-1]
    total = dots[0][...]
    for piece in dots[1:]:
        total = total + piece[...]
    rz0, dq, qw, wv = (total[i : i + 1, :] for i in range(4))
    alpha0 = rz0 / dq
    rz1 = alpha0 * alpha0 * qw - rz0
    grow = 1.0 + rz1 / rz0
    curve1 = grow * grow * dq - 2.0 * alpha0 * grow * qw + alpha0 * alpha0 * wv
    alpha1 = rz1 / curve1
    used = lane_index(1) < rows
    on_d = jnp.where(used, alpha0 + alpha1 * grow, 0.0)
    on_w = jnp.where(used, -alpha0 * alpha1, 0.0)
    pair = jnp.concatenate([on_d, on_w, jnp.zeros((6, LANES), F32)], axis=0)
    for i in range(coeffs.shape[0] // 8):
        coeffs[8 * i : 8 * i + 8, :] = pair


def late_kernel(n_near, n_far, exchange, coeffs, qv_high, qv_low, near_gram, far_gram, *refs):
    far, outs, gram = refs[:n_far], refs[n_far:-1], refs[-1]
    rows = near_gram.shape[1] // 2
    far_sum = None
    for slot in range(2):
        images = (qv_high[slot], qv_low[slot])
        term = product(images, split(columns_of(far, slot)), ((1,), (1,)))
        far_sum = term if slot == 0 else far_sum + term
    p, s = turned(coeffs, rows)
    if not exchange:
        gram = outs[0]
    for i in range(n_near):
        gram[i] = p * near_gram[i, 0:rows] + s * near_gram[i, rows : 2 * rows]
    d_part = far_gram[...]
    for i in range(n_far):
        there = slice(i * rows, (i + 1) * rows)
        both = jnp.concatenate([d_part[:, there], far_sum[:, there]], axis=1)
        gram[n_near + i] = p * both[0:rows] + s * both[rows : 2 * rows]
    if exchange:
        mine = lax.axis_index("nodes") ^ lax.axis_index("cols")
        for i in range(n_near + n_far):
            outs[i][...] = gram[mine ^ i]


def turned(coeffs, rows):
    table = jnp.concatenate([coeffs[0:8, :], jnp.zeros((LANES - 8, LANES), F32)], axis=0).T
    return [jnp.broadcast_to(table[0:rows, i : i + 1], (rows, LANES)) for i in range(2)]


def modes_kernel(coeffs, near, modes):
    rows = modes.shape[0]
    p, s = turned(coeffs, rows)
    for slot, plane in enumerate(slot_planes()):
        for k in range(CHUNKS):
            modes[:, plane_chunk(plane, k)] = (
                p * near[slot, 0:rows, chunk(k)] + s * near[slot, rows : 2 * rows, chunk(k)]
            )


def fifth_kernel(scale, n_sums, *refs):
    sums, coeffs_of, tile = refs[:n_sums], refs[n_sums:-1], refs[-1]
    rows = tile.shape[0]
    total = sums[0][...]
    for piece in sums[1:]:
        total = total + piece[...]
    mine = lax.axis_index("nodes") ^ lax.axis_index("cols")
    coeffs = coeffs_of[0][0:8, :]
    for i in range(1, n_sums):
        coeffs = jnp.where(mine == i, coeffs_of[i][0:8, :], coeffs)
    tile[...] = (
        coeffs[0:1, 0:rows] * total[:, 0:rows] + coeffs[1:2, 0:rows] * total[:, rows : 2 * rows]
    ) * scale


def call(kernel, name, args, shapes, scratch=(), space=pltpu.VMEM):
    shapes = [
        shape if isinstance(shape, jax.ShapeDtypeStruct) else jax.ShapeDtypeStruct(shape, F32)
        for shape in shapes
    ]
    return pl.pallas_call(
        kernel,
        out_shape=shapes,
        in_specs=[pl.BlockSpec(memory_space=space)] * len(args),
        out_specs=[pl.BlockSpec(memory_space=pltpu.VMEM)] * len(shapes),
        scratch_shapes=scratch,
        compiler_params=pltpu.CompilerParams(vmem_limit_bytes=KERNEL_BYTES),
        name=name,
    )(*args)


def neighbours(block, first):
    nodes, cols = lax.axis_size("nodes"), lax.axis_size("cols")
    route = []
    for n in range(nodes):
        other = n + 1 if n % 2 == first else n - 1
        for c in range(cols):
            here = n * cols + c
            if 0 <= other < nodes:
                route.append((here, other * cols + c))
            elif cols % 2 == 0:
                route.append((here, here ^ 1))
    return lax.ppermute(block, ("nodes", "cols"), route)


def swapped(block, axis, bit):
    return lax.ppermute(block, axis, [(i, i ^ bit) for i in range(lax.axis_size(axis))])


def on_device(forces, couplings, ground, precond):
    rows, length = forces.shape
    nodes, cols = lax.axis_size("nodes"), lax.axis_size("cols")
    ground = ground.reshape(1, length)
    bits = []
    while 2 ** len(bits) < cols:
        bits.append(2 ** len(bits))
    top = cols // 2

    def shared(block):
        held = {0: block}
        for bit in bits[:-1]:
            for key in list(held):
                held[key ^ bit] = swapped(held[key], "cols", bit)
        return [held[key] for key in range(max(top, 1))]

    field = (rows, PLANE)
    d_a, d_b = call(
        first_kernel,
        "first",
        [pltpu.with_memory_space_constraint(x, pltpu.HBM) for x in (forces, precond)],
        [field] * 2,
        [
            pltpu.VMEM((2, rows, PLANE), F32),
            pltpu.VMEM((2, CHUNKS, LANES, LANES), F32),
            pltpu.SemaphoreType.DMA((2, 2)),
        ],
        pltpu.HBM,
    )
    got_a, got_b = neighbours(d_a, 1), neighbours(d_b, 0)
    forces_far = swapped(forces, "cols", top)
    last = couplings[2:3, length - PLANE :]
    before_a, before_b = neighbours(last, 1), neighbours(last, 0)
    edges = (couplings, ground, before_a, before_b)
    q, w_a, w_b, w_both, near = call(
        second_kernel,
        "second",
        (*edges, precond, d_a, d_b, got_a, got_b),
        [(2,) + field, field, field, (2,) + field, (2, 2 * rows, PLANE)],
    )
    w_a, w_b, w_both, near, forces_far = lax.optimization_barrier(
        (w_a, w_b, w_both, near, forces_far)
    )
    next_a, next_b = neighbours(w_a, 1), neighbours(w_b, 0)
    far = swapped(w_both, "cols", top)
    near = shared(near)
    d_far, packed = call(
        other_kernel,
        "other",
        (forces_far, precond, forces, q, near[0]),
        [(2,) + field, (rows, LANES)],
    )
    next_a, next_b, d_far, near = lax.optimization_barrier((next_a, next_b, d_far, near))
    d_far = shared(d_far)
    v, dots = call(
        third_kernel,
        "third",
        (*edges, w_a, w_b, next_a, next_b, packed),
        [(2,) + field, (8, LANES)],
    )
    exchange = nodes == cols
    if exchange:
        dots = [dots] + [swapped(dots, "nodes", i) for i in range(1, nodes)]
    else:
        dots = [lax.psum(dots, "nodes")]
    halves = jax.ShapeDtypeStruct((2, 2 * rows, PLANE), jnp.bfloat16)
    qv_high, qv_low, near_gram = call(
        functools.partial(early_kernel, len(near)),
        "early",
        (q, v, *near),
        [halves, halves, (len(near), 2 * rows, 2 * rows)],
    )
    d_far, far = lax.optimization_barrier((d_far, far))
    (far_gram,) = call(
        far_kernel, "far", (qv_high, qv_low, *d_far), [(2 * rows, len(d_far) * rows)]
    )
    far, far_gram, *dots = lax.optimization_barrier((far, far_gram, *dots))
    far = shared(far)
    (coeffs,) = call(functools.partial(coeffs_kernel, rows), "coeffs", dots, [(rows + 8, LANES)])
    grams = call(
        functools.partial(late_kernel, len(near), len(d_far), exchange),
        "late",
        (coeffs, qv_high, qv_low, near_gram, far_gram, *far),
        [(rows, LANES)] * cols if exchange else [(cols, rows, LANES)],
        [pltpu.VMEM((cols, rows, LANES), F32)],
    )
    scale = 1.0 / (length * nodes)
    (modes,) = call(modes_kernel, "modes", (coeffs, near[0]), [(rows, length)])
    if exchange:
        theirs = [coeffs] + [swapped(coeffs, "cols", i) for i in range(1, cols)]
        sums = [grams[0]] + [swapped(grams[i], "nodes", i) for i in reversed(range(1, nodes))]
        (tile,) = call(
            functools.partial(fifth_kernel, scale, nodes),
            "fifth",
            (*sums, *theirs),
            [(rows, rows)],
        )
    else:
        gram = grams[0]
        every = lax.all_gather(coeffs, "cols")
        mine = lax.axis_index("cols")
        parts = []
        for i in range(cols):
            block = lax.dynamic_index_in_dim(gram, mine ^ i, 0, keepdims=False)
            parts.append(
                every[i, 0:1, 0:rows] * block[:, 0:rows]
                + every[i, 1:2, 0:rows] * block[:, rows : 2 * rows]
            )
        partial = jnp.concatenate(parts, axis=1) * scale
        tile = lax.psum_scatter(partial, "nodes", scatter_dimension=1, tiled=True)
    return (modes, tile)


def solution(mesh):
    in_specs = (
        P("cols", ("groups", "nodes")),
        P(None, ("groups", "nodes")),
        P(("groups", "nodes")),
        P(("groups", "nodes"), None, None),
    )
    out_specs = (P("cols", ("groups", "nodes")), P(("groups", "cols"), "nodes"))
    return jax.shard_map(
        on_device, mesh=mesh, in_specs=in_specs, out_specs=out_specs, check_vma=False
    )
```

```python
import functools

import jax
import jax.numpy as jnp
from jax import lax
from jax.experimental import pallas as pl
from jax.experimental.pallas import tpu as pltpu
from jax.sharding import PartitionSpec as P

GRID_X = 32
GRID_Y = 32
PLANE = GRID_X * GRID_Y
LANES = 128
CHUNKS = PLANE // LANES
F32 = jnp.float32
KERNEL_BYTES = 8 * 2**20


def slot_planes():
    odd = lax.rem(lax.axis_index("nodes"), 2)
    return odd, 1 - odd


def split(x):
    high = x.astype(jnp.bfloat16)
    return high, (x - high.astype(F32)).astype(jnp.bfloat16)


def product(left, right, dims):
    left_high, left_low = left
    right_high, right_low = right
    dot = functools.partial(
        lax.dot_general, dimension_numbers=(dims, ((), ())), preferred_element_type=F32
    )
    return dot(left_high, right_high) + (
        dot(left_low, right_high) + dot(left_high, right_low)
    )


def block_product(x, matrix):
    return product(split(x), split(matrix), ((1,), (0,)))


def chunk(k):
    return slice(k * LANES, (k + 1) * LANES)


def plane_chunk(plane, k):
    return pl.ds(pl.multiple_of(plane * PLANE + k * LANES, LANES), LANES)


def lane_index(rows=8):
    return lax.broadcasted_iota(jnp.int32, (rows, LANES), 1)


def ahead_row(here, after):
    lane = lax.broadcasted_iota(jnp.int32, here.shape, here.ndim - 1)
    mixed = here if after is None else jnp.where(lane < GRID_X, after, here)
    return pltpu.roll(mixed, LANES - GRID_X, mixed.ndim - 1)


def behind_row(before, here):
    lane = lax.broadcasted_iota(jnp.int32, here.shape, here.ndim - 1)
    mixed = here if before is None else jnp.where(lane >= LANES - GRID_X, before, here)
    return pltpu.roll(mixed, GRID_X, mixed.ndim - 1)


def plane_springs(couplings, ground, plane, middle, crossing, meets):
    lane = lane_index()
    inside_x = lane % GRID_X < GRID_X - 1

    def row(ref, index, k):
        return jnp.broadcast_to(ref[index : index + 1, plane_chunk(plane, k)], (8, LANES))

    along_y = []
    for k in range(CHUNKS):
        spring = row(couplings, 1, k)
        if k == CHUNKS - 1:
            spring = jnp.where(lane < LANES - GRID_X, spring, 0.0)
        along_y.append(spring)
    result = []
    for k in range(CHUNKS):
        right = jnp.where(inside_x, row(couplings, 0, k), 0.0)
        left = pltpu.roll(right, 1, 1)
        up = along_y[k]
        before = along_y[k - 1] if k else jnp.zeros_like(up)
        down = behind_row(before, up)
        diag = row(ground, 0, k) + (right + left) + (up + down) + (middle[k] + crossing[k])
        halo = jnp.where(meets, crossing[k], 0.0)
        result.append((diag, right, left, up, down, middle[k], halo))
    return result


def all_springs(couplings, ground, got):
    def row_before(slot, k):
        return jnp.broadcast_to(got[slot][0:1, chunk(k)], (8, LANES))

    place, count = lax.axis_index("nodes"), lax.axis_size("nodes")
    odd = lax.rem(place, 2)
    own, mid = [], []
    for k in range(CHUNKS):
        own.append(
            jnp.broadcast_to(
                couplings[2:3, PLANE + k * LANES : PLANE + (k + 1) * LANES], (8, LANES)
            )
        )
        mid.append(jnp.broadcast_to(couplings[2:3, chunk(k)], (8, LANES)))
    result = []
    for slot, plane in enumerate(slot_planes()):
        below = odd == slot
        meets = jnp.where(below, place > 0, place < count - 1)
        crossing = [
            jnp.where(
                below,
                jnp.where(place > 0, row_before(slot, k), 0.0),
                own[k],
            )
            for k in range(CHUNKS)
        ]
        result.append(plane_springs(couplings, ground, plane, mid, crossing, meets))
    return result


def stiff_chunk(springs, k, field, other, halo, rows):
    def load(ref, index):
        return ref[0:rows, chunk(index)].reshape(rows // 8, 8, LANES)

    diag, right, left, up, down, middle, crossing = springs[k]
    here = load(field, k)
    before = load(field, k - 1) if k else None
    after = load(field, k + 1) if k < CHUNKS - 1 else None
    result = diag * here
    result = result - right * pltpu.roll(here, LANES - 1, 2)
    result = result - left * pltpu.roll(here, 1, 2)
    result = result - up * ahead_row(here, after)
    result = result - down * behind_row(before, here)
    result = result - middle * load(other, k)
    result = result - crossing * load(halo, k)
    return result.reshape(rows, LANES)


def first_kernel(forces, precond, out_a, out_b, field, matrices, sems):
    copies = []
    for slot, plane in enumerate(slot_planes()):
        here = pl.ds(pl.multiple_of(plane * PLANE, PLANE), PLANE)
        copies.append(
            (
                pltpu.make_async_copy(forces.at[:, here], field.at[slot], sems.at[slot, 0]),
                pltpu.make_async_copy(
                    precond.at[pl.ds(plane * CHUNKS, CHUNKS)], matrices.at[slot], sems.at[slot, 1]
                ),
            )
        )
    for pair in copies:
        for copy in pair:
            copy.start()
    for slot, out in enumerate((out_a, out_b)):
        for copy in copies[slot]:
            copy.wait()
        for k in range(CHUNKS):
            out[:, chunk(k)] = block_product(field[slot, :, chunk(k)], matrices[slot, k])


def place_sums(packed, first, sums):
    lane = lane_index(packed.shape[0])
    for index, value in enumerate(sums):
        total = jnp.sum(value, axis=1, keepdims=True)
        packed = jnp.where(lane == first + index, total, packed)
    return packed


def other_kernel(forces_far, precond, forces, q, near, d_far, packed):
    rows = forces.shape[0]
    sums = [jnp.zeros((rows, LANES), F32) for _ in range(3)]
    for slot, plane in enumerate(slot_planes()):
        for k in range(CHUNKS):
            d_far[slot, :, chunk(k)] = block_product(
                forces_far[:, plane_chunk(plane, k)], precond[plane * CHUNKS + k]
            )
            d_here = near[slot, 0:rows, chunk(k)]
            q_here = q[slot, :, chunk(k)]
            sums[0] += forces[:, plane_chunk(plane, k)] * d_here
            sums[1] += d_here * q_here
            sums[2] += q_here * near[slot, rows : 2 * rows, chunk(k)]
    packed[...] = place_sums(jnp.zeros((rows, LANES), F32), 0, sums)


def second_kernel(couplings, ground, before_a, before_b, precond, d_a, d_b, got_a, got_b, q, w_a, w_b, w_both, near):
    rows = w_a.shape[0]
    springs = all_springs(couplings, ground, (before_a, before_b))
    fields = (d_a, d_b)
    for slot, plane in enumerate(slot_planes()):
        for k in range(CHUNKS):
            image = stiff_chunk(
                springs[slot], k, fields[slot], fields[1 - slot], (got_a, got_b)[slot], rows
            )
            q[slot, :, chunk(k)] = image
            w = block_product(image, precond[plane * CHUNKS + k])
            (w_a, w_b)[slot][:, chunk(k)] = w
            w_both[slot, :, chunk(k)] = w
            near[slot, 0:rows, chunk(k)] = fields[slot][:, chunk(k)]
            near[slot, rows : 2 * rows, chunk(k)] = w


def third_kernel(couplings, ground, before_a, before_b, w_a, w_b, next_a, next_b, packed, v, dots):
    rows = w_a.shape[0]
    springs = all_springs(couplings, ground, (before_a, before_b))
    fields = (w_a, w_b)
    total = jnp.zeros((rows, LANES), F32)
    for slot in range(2):
        for k in range(CHUNKS):
            image = stiff_chunk(
                springs[slot], k, fields[slot], fields[1 - slot], (next_a, next_b)[slot], rows
            )
            v[slot, :, chunk(k)] = image
            total += fields[slot][:, chunk(k)] * image
    values = place_sums(packed[...], 3, [total])
    if rows < LANES:
        values = jnp.concatenate([values, jnp.zeros((LANES - rows, LANES), F32)], axis=0)
    dots[...] = values.T[0:8, :]


def columns_of(fields, slot):
    return jnp.concatenate([field[slot] for field in fields], axis=0)


def early_kernel(n_near, q, v, *refs):
    near, (qv_high, qv_low, near_gram) = refs[:n_near], refs[n_near:]
    sums = [None] * n_near
    for slot in range(2):
        images = split(jnp.concatenate([q[slot], v[slot]], axis=0))
        qv_high[slot], qv_low[slot] = images
        for i in range(n_near):
            term = product(images, split(near[i][slot]), ((1,), (1,)))
            sums[i] = term if slot == 0 else sums[i] + term
    for i in range(n_near):
        near_gram[i] = sums[i]


def far_kernel(qv_high, qv_low, *refs):
    d_far, far_gram = refs[:-1], refs[-1]
    total = None
    for slot in range(2):
        images = (qv_high[slot], qv_low[slot])
        term = product(images, split(columns_of(d_far, slot)), ((1,), (1,)))
        total = term if slot == 0 else total + term
    far_gram[...] = total


def coeffs_kernel(rows, *refs):
    dots, coeffs = refs[:-1], refs[-1]
    total = dots[0][...]
    for piece in dots[1:]:
        total = total + piece[...]
    rz0, dq, qw, wv = (total[i : i + 1, :] for i in range(4))
    alpha0 = rz0 / dq
    rz1 = alpha0 * alpha0 * qw - rz0
    grow = 1.0 + rz1 / rz0
    curve1 = grow * grow * dq - 2.0 * alpha0 * grow * qw + alpha0 * alpha0 * wv
    alpha1 = rz1 / curve1
    used = lane_index(1) < rows
    on_d = jnp.where(used, alpha0 + alpha1 * grow, 0.0)
    on_w = jnp.where(used, -alpha0 * alpha1, 0.0)
    pair = jnp.concatenate([on_d, on_w, jnp.zeros((6, LANES), F32)], axis=0)
    for i in range(coeffs.shape[0] // 8):
        coeffs[8 * i : 8 * i + 8, :] = pair


def late_kernel(n_near, n_far, exchange, coeffs, qv_high, qv_low, near_gram, far_gram, *refs):
    far, outs, gram = refs[:n_far], refs[n_far:-1], refs[-1]
    rows = near_gram.shape[1] // 2
    far_sum = None
    for slot in range(2):
        images = (qv_high[slot], qv_low[slot])
        term = product(images, split(columns_of(far, slot)), ((1,), (1,)))
        far_sum = term if slot == 0 else far_sum + term
    p, s = turned(coeffs, rows)
    if not exchange:
        gram = outs[0]
    for i in range(n_near):
        gram[i] = p * near_gram[i, 0:rows] + s * near_gram[i, rows : 2 * rows]
    d_part = far_gram[...]
    for i in range(n_far):
        there = slice(i * rows, (i + 1) * rows)
        both = jnp.concatenate([d_part[:, there], far_sum[:, there]], axis=1)
        gram[n_near + i] = p * both[0:rows] + s * both[rows : 2 * rows]
    if exchange:
        mine = lax.axis_index("nodes") ^ lax.axis_index("cols")
        for i in range(n_near + n_far):
            outs[i][...] = gram[mine ^ i]


def turned(coeffs, rows):
    table = jnp.concatenate([coeffs[0:8, :], jnp.zeros((LANES - 8, LANES), F32)], axis=0).T
    return [jnp.broadcast_to(table[0:rows, i : i + 1], (rows, LANES)) for i in range(2)]


def modes_kernel(coeffs, near, modes):
    rows = modes.shape[0]
    p, s = turned(coeffs, rows)
    for slot, plane in enumerate(slot_planes()):
        for k in range(CHUNKS):
            modes[:, plane_chunk(plane, k)] = (
                p * near[slot, 0:rows, chunk(k)] + s * near[slot, rows : 2 * rows, chunk(k)]
            )


def fifth_kernel(scale, n_sums, *refs):
    sums, coeffs_of, tile = refs[:n_sums], refs[n_sums:-1], refs[-1]
    rows = tile.shape[0]
    total = sums[0][...]
    for piece in sums[1:]:
        total = total + piece[...]
    mine = lax.axis_index("nodes") ^ lax.axis_index("cols")
    coeffs = coeffs_of[0][0:8, :]
    for i in range(1, n_sums):
        coeffs = jnp.where(mine == i, coeffs_of[i][0:8, :], coeffs)
    tile[...] = (
        coeffs[0:1, 0:rows] * total[:, 0:rows] + coeffs[1:2, 0:rows] * total[:, rows : 2 * rows]
    ) * scale


def call(kernel, name, args, shapes, scratch=(), space=pltpu.VMEM):
    shapes = [
        shape if isinstance(shape, jax.ShapeDtypeStruct) else jax.ShapeDtypeStruct(shape, F32)
        for shape in shapes
    ]
    return pl.pallas_call(
        kernel,
        out_shape=shapes,
        in_specs=[pl.BlockSpec(memory_space=space)] * len(args),
        out_specs=[pl.BlockSpec(memory_space=pltpu.VMEM)] * len(shapes),
        scratch_shapes=scratch,
        compiler_params=pltpu.CompilerParams(vmem_limit_bytes=KERNEL_BYTES),
        name=name,
    )(*args)


def neighbours(block, first):
    nodes, cols = lax.axis_size("nodes"), lax.axis_size("cols")
    route = []
    for n in range(nodes):
        other = n + 1 if n % 2 == first else n - 1
        for c in range(cols):
            here = n * cols + c
            if 0 <= other < nodes:
                route.append((here, other * cols + c))
            elif cols % 2 == 0:
                route.append((here, here ^ 1))
    return lax.ppermute(block, ("nodes", "cols"), route)


def swapped(block, axis, bit):
    return lax.ppermute(block, axis, [(i, i ^ bit) for i in range(lax.axis_size(axis))])


def on_device(forces, couplings, ground, precond):
    rows, length = forces.shape
    nodes, cols = lax.axis_size("nodes"), lax.axis_size("cols")
    ground = ground.reshape(1, length)
    bits = []
    while 2 ** len(bits) < cols:
        bits.append(2 ** len(bits))
    top = cols // 2

    def shared(block):
        held = {0: block}
        for bit in bits[:-1]:
            for key in list(held):
                held[key ^ bit] = swapped(held[key], "cols", bit)
        return [held[key] for key in range(max(top, 1))]

    field = (rows, PLANE)
    d_a, d_b = call(
        first_kernel,
        "first",
        [pltpu.with_memory_space_constraint(x, pltpu.HBM) for x in (forces, precond)],
        [field] * 2,
        [
            pltpu.VMEM((2, rows, PLANE), F32),
            pltpu.VMEM((2, CHUNKS, LANES, LANES), F32),
            pltpu.SemaphoreType.DMA((2, 2)),
        ],
        pltpu.HBM,
    )
    got_a, got_b = neighbours(d_a, 1), neighbours(d_b, 0)
    forces_far = swapped(forces, "cols", top)
    last = couplings[2:3, length - PLANE :]
    before_a, before_b = neighbours(last, 1), neighbours(last, 0)
    edges = (couplings, ground, before_a, before_b)
    q, w_a, w_b, w_both, near = call(
        second_kernel,
        "second",
        (*edges, precond, d_a, d_b, got_a, got_b),
        [(2,) + field, field, field, (2,) + field, (2, 2 * rows, PLANE)],
    )
    w_a, w_b, w_both, near, forces_far = lax.optimization_barrier(
        (w_a, w_b, w_both, near, forces_far)
    )
    next_a, next_b = neighbours(w_a, 1), neighbours(w_b, 0)
    far = swapped(w_both, "cols", top)
    near = shared(near)
    d_far, packed = call(
        other_kernel,
        "other",
        (forces_far, precond, forces, q, near[0]),
        [(2,) + field, (rows, LANES)],
    )
    next_a, next_b, d_far, near = lax.optimization_barrier((next_a, next_b, d_far, near))
    d_far = shared(d_far)
    v, dots = call(
        third_kernel,
        "third",
        (*edges, w_a, w_b, next_a, next_b, packed),
        [(2,) + field, (8, LANES)],
    )
    exchange = nodes == cols
    if exchange:
        dots = [dots] + [swapped(dots, "nodes", i) for i in range(1, nodes)]
    else:
        dots = [lax.psum(dots, "nodes")]
    halves = jax.ShapeDtypeStruct((2, 2 * rows, PLANE), jnp.bfloat16)
    qv_high, qv_low, near_gram = call(
        functools.partial(early_kernel, len(near)),
        "early",
        (q, v, *near),
        [halves, halves, (len(near), 2 * rows, 2 * rows)],
    )
    d_far, far = lax.optimization_barrier((d_far, far))
    (far_gram,) = call(
        far_kernel, "far", (qv_high, qv_low, *d_far), [(2 * rows, len(d_far) * rows)]
    )
    far, far_gram, *dots = lax.optimization_barrier((far, far_gram, *dots))
    far = shared(far)
    (coeffs,) = call(functools.partial(coeffs_kernel, rows), "coeffs", dots, [(rows + 8, LANES)])
    grams = call(
        functools.partial(late_kernel, len(near), len(d_far), exchange),
        "late",
        (coeffs, qv_high, qv_low, near_gram, far_gram, *far),
        [(rows, LANES)] * cols if exchange else [(cols, rows, LANES)],
        [pltpu.VMEM((cols, rows, LANES), F32)],
    )
    scale = 1.0 / (length * nodes)
    (modes,) = call(modes_kernel, "modes", (coeffs, near[0]), [(rows, length)])
    if exchange:
        held = {0: coeffs}
        for bit in reversed(bits):
            for key in list(held):
                held[key ^ bit] = swapped(held[key] if key == 0 else held[key][0:8], "cols", bit)
        theirs = [held[key] for key in range(cols)]
        sums = [grams[0]] + [swapped(grams[i], "nodes", i) for i in reversed(range(1, nodes))]
        (tile,) = call(
            functools.partial(fifth_kernel, scale, nodes),
            "fifth",
            (*sums, *theirs),
            [(rows, rows)],
        )
    else:
        gram = grams[0]
        every = lax.all_gather(coeffs, "cols")
        mine = lax.axis_index("cols")
        parts = []
        for i in range(cols):
            block = lax.dynamic_index_in_dim(gram, mine ^ i, 0, keepdims=False)
            parts.append(
                every[i, 0:1, 0:rows] * block[:, 0:rows]
                + every[i, 1:2, 0:rows] * block[:, rows : 2 * rows]
            )
        partial = jnp.concatenate(parts, axis=1) * scale
        tile = lax.psum_scatter(partial, "nodes", scatter_dimension=1, tiled=True)
    return (modes, tile)


def solution(mesh):
    in_specs = (
        P("cols", ("groups", "nodes")),
        P(None, ("groups", "nodes")),
        P(("groups", "nodes")),
        P(("groups", "nodes"), None, None),
    )
    out_specs = (P("cols", ("groups", "nodes")), P(("groups", "cols"), "nodes"))
    return jax.shard_map(
        on_device, mesh=mesh, in_specs=in_specs, out_specs=out_specs, check_vma=False
    )
```

```python
import functools

import jax
import jax.numpy as jnp
from jax import lax
from jax.experimental import pallas as pl
from jax.experimental.pallas import tpu as pltpu
from jax.sharding import PartitionSpec as P

GRID_X = 32
GRID_Y = 32
PLANE = GRID_X * GRID_Y
LANES = 128
CHUNKS = PLANE // LANES
F32 = jnp.float32
KERNEL_BYTES = 8 * 2**20


def slot_planes():
    odd = lax.rem(lax.axis_index("nodes"), 2)
    return odd, 1 - odd


def split(x):
    high = x.astype(jnp.bfloat16)
    return high, (x - high.astype(F32)).astype(jnp.bfloat16)


def product(left, right, dims):
    left_high, left_low = left
    right_high, right_low = right
    dot = functools.partial(
        lax.dot_general, dimension_numbers=(dims, ((), ())), preferred_element_type=F32
    )
    return dot(left_high, right_high) + (
        dot(left_low, right_high) + dot(left_high, right_low)
    )


def block_product(x, matrix):
    return product(split(x), split(matrix), ((1,), (0,)))


def chunk(k):
    return slice(k * LANES, (k + 1) * LANES)


def plane_chunk(plane, k):
    return pl.ds(pl.multiple_of(plane * PLANE + k * LANES, LANES), LANES)


def lane_index(rows=8):
    return lax.broadcasted_iota(jnp.int32, (rows, LANES), 1)


def ahead_row(here, after):
    lane = lax.broadcasted_iota(jnp.int32, here.shape, here.ndim - 1)
    mixed = here if after is None else jnp.where(lane < GRID_X, after, here)
    return pltpu.roll(mixed, LANES - GRID_X, mixed.ndim - 1)


def behind_row(before, here):
    lane = lax.broadcasted_iota(jnp.int32, here.shape, here.ndim - 1)
    mixed = here if before is None else jnp.where(lane >= LANES - GRID_X, before, here)
    return pltpu.roll(mixed, GRID_X, mixed.ndim - 1)


def plane_springs(couplings, ground, plane, middle, crossing, meets):
    lane = lane_index()
    inside_x = lane % GRID_X < GRID_X - 1

    def row(ref, index, k):
        return jnp.broadcast_to(ref[index : index + 1, plane_chunk(plane, k)], (8, LANES))

    along_y = []
    for k in range(CHUNKS):
        spring = row(couplings, 1, k)
        if k == CHUNKS - 1:
            spring = jnp.where(lane < LANES - GRID_X, spring, 0.0)
        along_y.append(spring)
    result = []
    for k in range(CHUNKS):
        right = jnp.where(inside_x, row(couplings, 0, k), 0.0)
        left = pltpu.roll(right, 1, 1)
        up = along_y[k]
        before = along_y[k - 1] if k else jnp.zeros_like(up)
        down = behind_row(before, up)
        diag = row(ground, 0, k) + (right + left) + (up + down) + (middle[k] + crossing[k])
        halo = jnp.where(meets, crossing[k], 0.0)
        result.append((diag, right, left, up, down, middle[k], halo))
    return result


def all_springs(couplings, ground, got):
    def row_before(slot, k):
        return jnp.broadcast_to(got[slot][0:1, chunk(k)], (8, LANES))

    place, count = lax.axis_index("nodes"), lax.axis_size("nodes")
    odd = lax.rem(place, 2)
    own, mid = [], []
    for k in range(CHUNKS):
        own.append(
            jnp.broadcast_to(
                couplings[2:3, PLANE + k * LANES : PLANE + (k + 1) * LANES], (8, LANES)
            )
        )
        mid.append(jnp.broadcast_to(couplings[2:3, chunk(k)], (8, LANES)))
    result = []
    for slot, plane in enumerate(slot_planes()):
        below = odd == slot
        meets = jnp.where(below, place > 0, place < count - 1)
        crossing = [
            jnp.where(
                below,
                jnp.where(place > 0, row_before(slot, k), 0.0),
                own[k],
            )
            for k in range(CHUNKS)
        ]
        result.append(plane_springs(couplings, ground, plane, mid, crossing, meets))
    return result


def stiff_chunk(springs, k, field, other, halo, rows):
    def load(ref, index):
        return ref[0:rows, chunk(index)].reshape(rows // 8, 8, LANES)

    diag, right, left, up, down, middle, crossing = springs[k]
    here = load(field, k)
    before = load(field, k - 1) if k else None
    after = load(field, k + 1) if k < CHUNKS - 1 else None
    result = diag * here
    result = result - right * pltpu.roll(here, LANES - 1, 2)
    result = result - left * pltpu.roll(here, 1, 2)
    result = result - up * ahead_row(here, after)
    result = result - down * behind_row(before, here)
    result = result - middle * load(other, k)
    if halo is not None:
        result = result - crossing * load(halo, k)
    return result.reshape(rows, LANES)


def first_kernel(forces, precond, out_a, out_b, field, matrices, sems):
    copies = []
    for slot, plane in enumerate(slot_planes()):
        here = pl.ds(pl.multiple_of(plane * PLANE, PLANE), PLANE)
        copies.append(
            (
                pltpu.make_async_copy(forces.at[:, here], field.at[slot], sems.at[slot, 0]),
                pltpu.make_async_copy(
                    precond.at[pl.ds(plane * CHUNKS, CHUNKS)], matrices.at[slot], sems.at[slot, 1]
                ),
            )
        )
    for pair in copies:
        for copy in pair:
            copy.start()
    for slot, out in enumerate((out_a, out_b)):
        for copy in copies[slot]:
            copy.wait()
        for k in range(CHUNKS):
            out[:, chunk(k)] = block_product(field[slot, :, chunk(k)], matrices[slot, k])


def place_sums(packed, first, sums):
    lane = lane_index(packed.shape[0])
    for index, value in enumerate(sums):
        total = jnp.sum(value, axis=1, keepdims=True)
        packed = jnp.where(lane == first + index, total, packed)
    return packed


def other_kernel(
    forces_far, precond, forces, q, near, couplings, ground, before_a, before_b, w_a, w_b, d_far, local, packed
):
    rows = forces.shape[0]
    springs = all_springs(couplings, ground, (before_a, before_b))
    fields = (w_a, w_b)
    sums = [jnp.zeros((rows, LANES), F32) for _ in range(4)]
    for slot, plane in enumerate(slot_planes()):
        for k in range(CHUNKS):
            d_far[slot, :, chunk(k)] = block_product(
                forces_far[:, plane_chunk(plane, k)], precond[plane * CHUNKS + k]
            )
            d_here = near[slot, 0:rows, chunk(k)]
            q_here = q[slot, :, chunk(k)]
            sums[0] += forces[:, plane_chunk(plane, k)] * d_here
            sums[1] += d_here * q_here
            w_here = near[slot, rows : 2 * rows, chunk(k)]
            sums[2] += q_here * w_here
            image = stiff_chunk(springs[slot], k, fields[slot], fields[1 - slot], None, rows)
            local[slot, :, chunk(k)] = image
            sums[3] += w_here * image
    packed[...] = place_sums(jnp.zeros((rows, LANES), F32), 0, sums)


def second_kernel(couplings, ground, before_a, before_b, precond, d_a, d_b, got_a, got_b, q, w_a, w_b, w_both, near):
    rows = w_a.shape[0]
    springs = all_springs(couplings, ground, (before_a, before_b))
    fields = (d_a, d_b)
    for slot, plane in enumerate(slot_planes()):
        for k in range(CHUNKS):
            image = stiff_chunk(
                springs[slot], k, fields[slot], fields[1 - slot], (got_a, got_b)[slot], rows
            )
            q[slot, :, chunk(k)] = image
            w = block_product(image, precond[plane * CHUNKS + k])
            (w_a, w_b)[slot][:, chunk(k)] = w
            w_both[slot, :, chunk(k)] = w
            near[slot, 0:rows, chunk(k)] = fields[slot][:, chunk(k)]
            near[slot, rows : 2 * rows, chunk(k)] = w


def third_kernel(couplings, ground, before_a, before_b, w_a, w_b, next_a, next_b, local, packed, v, dots):
    rows = w_a.shape[0]
    springs = all_springs(couplings, ground, (before_a, before_b))
    total = jnp.zeros((rows // 8, 8, LANES), F32)
    for slot, (here, halo) in enumerate(((w_a, next_a), (w_b, next_b))):
        for k in range(CHUNKS):
            term = springs[slot][k][6] * halo[:, chunk(k)].reshape(rows // 8, 8, LANES)
            v[slot, :, chunk(k)] = local[slot, :, chunk(k)] - term.reshape(rows, LANES)
            total += here[:, chunk(k)].reshape(rows // 8, 8, LANES) * term
    crossing = jnp.sum(total.reshape(rows, LANES), axis=1, keepdims=True)
    values = packed[...] - jnp.where(lane_index(rows) == 3, crossing, 0.0)
    if rows < LANES:
        values = jnp.concatenate([values, jnp.zeros((LANES - rows, LANES), F32)], axis=0)
    dots[...] = values.T[0:8, :]


def columns_of(fields, slot):
    return jnp.concatenate([field[slot] for field in fields], axis=0)


def early_kernel(n_near, q, v, d_far, *refs):
    near, (qv_high, qv_low, near_gram, own_far) = refs[:n_near], refs[n_near:]
    far_sum = None
    sums = [None] * n_near
    for slot in range(2):
        images = split(jnp.concatenate([q[slot], v[slot]], axis=0))
        qv_high[slot], qv_low[slot] = images
        for i in range(n_near):
            term = product(images, split(near[i][slot]), ((1,), (1,)))
            sums[i] = term if slot == 0 else sums[i] + term
        term = product(images, split(d_far[slot]), ((1,), (1,)))
        far_sum = term if slot == 0 else far_sum + term
    own_far[...] = far_sum
    for i in range(n_near):
        near_gram[i] = sums[i]


def far_kernel(qv_high, qv_low, *refs):
    d_far, far_gram = refs[:-1], refs[-1]
    total = None
    for slot in range(2):
        images = (qv_high[slot], qv_low[slot])
        term = product(images, split(columns_of(d_far, slot)), ((1,), (1,)))
        total = term if slot == 0 else total + term
    far_gram[...] = total


def coeffs_kernel(rows, *refs):
    dots, coeffs = refs[:-1], refs[-1]
    total = dots[0][...]
    for piece in dots[1:]:
        total = total + piece[...]
    rz0, dq, qw, wv = (total[i : i + 1, :] for i in range(4))
    alpha0 = rz0 / dq
    rz1 = alpha0 * alpha0 * qw - rz0
    grow = 1.0 + rz1 / rz0
    curve1 = grow * grow * dq - 2.0 * alpha0 * grow * qw + alpha0 * alpha0 * wv
    alpha1 = rz1 / curve1
    used = lane_index(1) < rows
    on_d = jnp.where(used, alpha0 + alpha1 * grow, 0.0)
    on_w = jnp.where(used, -alpha0 * alpha1, 0.0)
    pair = jnp.concatenate([on_d, on_w, jnp.zeros((6, LANES), F32)], axis=0)
    for i in range(coeffs.shape[0] // 8):
        coeffs[8 * i : 8 * i + 8, :] = pair


def late_kernel(n_near, n_far, exchange, coeffs, qv_high, qv_low, near_gram, own_far, far_gram, *refs):
    far, outs, gram = refs[:n_far], refs[n_far:-1], refs[-1]
    rows = near_gram.shape[1] // 2
    far_sum = None
    for slot in range(2):
        images = (qv_high[slot], qv_low[slot])
        term = product(images, split(columns_of(far, slot)), ((1,), (1,)))
        far_sum = term if slot == 0 else far_sum + term
    p, s = turned(coeffs, rows)
    if not exchange:
        gram = outs[0]
    for i in range(n_near):
        gram[i] = p * near_gram[i, 0:rows] + s * near_gram[i, rows : 2 * rows]
    d_part = [own_far[...]] + [far_gram[:, i * rows : (i + 1) * rows] for i in range(n_far - 1)]
    for i in range(n_far):
        both = jnp.concatenate([d_part[i], far_sum[:, i * rows : (i + 1) * rows]], axis=1)
        gram[n_near + i] = p * both[0:rows] + s * both[rows : 2 * rows]
    if exchange:
        mine = lax.axis_index("nodes") ^ lax.axis_index("cols")
        for i in range(n_near + n_far):
            outs[i][...] = gram[mine ^ i]


def turned(coeffs, rows):
    table = jnp.concatenate([coeffs[0:8, :], jnp.zeros((LANES - 8, LANES), F32)], axis=0).T
    return [jnp.broadcast_to(table[0:rows, i : i + 1], (rows, LANES)) for i in range(2)]


def modes_kernel(coeffs, near, modes):
    rows = modes.shape[0]
    p, s = turned(coeffs, rows)
    for slot, plane in enumerate(slot_planes()):
        for k in range(CHUNKS):
            modes[:, plane_chunk(plane, k)] = (
                p * near[slot, 0:rows, chunk(k)] + s * near[slot, rows : 2 * rows, chunk(k)]
            )


def fifth_kernel(scale, n_sums, *refs):
    sums, coeffs_of, tile = refs[:n_sums], refs[n_sums:-1], refs[-1]
    rows = tile.shape[0]
    total = sums[0][...]
    for piece in sums[1:]:
        total = total + piece[...]
    mine = lax.axis_index("nodes") ^ lax.axis_index("cols")
    coeffs = coeffs_of[0][0:8, :]
    for i in range(1, n_sums):
        coeffs = jnp.where(mine == i, coeffs_of[i][0:8, :], coeffs)
    tile[...] = (
        coeffs[0:1, 0:rows] * total[:, 0:rows] + coeffs[1:2, 0:rows] * total[:, rows : 2 * rows]
    ) * scale


def call(kernel, name, args, shapes, scratch=(), space=pltpu.VMEM):
    shapes = [
        shape if isinstance(shape, jax.ShapeDtypeStruct) else jax.ShapeDtypeStruct(shape, F32)
        for shape in shapes
    ]
    return pl.pallas_call(
        kernel,
        out_shape=shapes,
        in_specs=[pl.BlockSpec(memory_space=space)] * len(args),
        out_specs=[pl.BlockSpec(memory_space=pltpu.VMEM)] * len(shapes),
        scratch_shapes=scratch,
        compiler_params=pltpu.CompilerParams(vmem_limit_bytes=KERNEL_BYTES),
        name=name,
    )(*args)


def neighbours(block, first):
    nodes, cols = lax.axis_size("nodes"), lax.axis_size("cols")
    route = []
    for n in range(nodes):
        other = n + 1 if n % 2 == first else n - 1
        for c in range(cols):
            here = n * cols + c
            if 0 <= other < nodes:
                route.append((here, other * cols + c))
            elif cols % 2 == 0:
                route.append((here, here ^ 1))
    return lax.ppermute(block, ("nodes", "cols"), route)


def swapped(block, axis, bit):
    return lax.ppermute(block, axis, [(i, i ^ bit) for i in range(lax.axis_size(axis))])


def on_device(forces, couplings, ground, precond):
    rows, length = forces.shape
    nodes, cols = lax.axis_size("nodes"), lax.axis_size("cols")
    ground = ground.reshape(1, length)
    bits = []
    while 2 ** len(bits) < cols:
        bits.append(2 ** len(bits))
    top = cols // 2

    def shared(block):
        held = {0: block}
        for bit in bits[:-1]:
            for key in list(held):
                held[key ^ bit] = swapped(held[key], "cols", bit)
        return [held[key] for key in range(max(top, 1))]

    field = (rows, PLANE)
    d_a, d_b = call(
        first_kernel,
        "first",
        [pltpu.with_memory_space_constraint(x, pltpu.HBM) for x in (forces, precond)],
        [field] * 2,
        [
            pltpu.VMEM((2, rows, PLANE), F32),
            pltpu.VMEM((2, CHUNKS, LANES, LANES), F32),
            pltpu.SemaphoreType.DMA((2, 2)),
        ],
        pltpu.HBM,
    )
    got_a, got_b = neighbours(d_a, 1), neighbours(d_b, 0)
    forces_far = swapped(forces, "cols", top)
    last = couplings[2:3, length - PLANE :]
    before_a, before_b = neighbours(last, 1), neighbours(last, 0)
    edges = (couplings, ground, before_a, before_b)
    q, w_a, w_b, w_both, near = call(
        second_kernel,
        "second",
        (*edges, precond, d_a, d_b, got_a, got_b),
        [(2,) + field, field, field, (2,) + field, (2, 2 * rows, PLANE)],
    )
    w_a, w_b, w_both, near, forces_far = lax.optimization_barrier(
        (w_a, w_b, w_both, near, forces_far)
    )
    next_a, next_b = neighbours(w_a, 1), neighbours(w_b, 0)
    far = swapped(w_both, "cols", top)
    near = shared(near)
    d_far, local, packed = call(
        other_kernel,
        "other",
        (forces_far, precond, forces, q, near[0], *edges, w_a, w_b),
        [(2,) + field, (2,) + field, (rows, LANES)],
    )
    next_a, next_b, d_far, near = lax.optimization_barrier((next_a, next_b, d_far, near))
    d_far = shared(d_far)
    v, dots = call(
        third_kernel,
        "third",
        (*edges, w_a, w_b, next_a, next_b, local, packed),
        [(2,) + field, (8, LANES)],
    )
    exchange = nodes == cols
    if exchange:
        dots = [dots] + [swapped(dots, "nodes", i) for i in range(1, nodes)]
    else:
        dots = [lax.psum(dots, "nodes")]
    halves = jax.ShapeDtypeStruct((2, 2 * rows, PLANE), jnp.bfloat16)
    qv_high, qv_low, near_gram, own_far = call(
        functools.partial(early_kernel, len(near)),
        "early",
        (q, v, d_far[0], *near),
        [halves, halves, (len(near), 2 * rows, 2 * rows), (2 * rows, rows)],
    )
    d_far, far = lax.optimization_barrier((d_far, far))
    (far_gram,) = call(
        far_kernel, "far", (qv_high, qv_low, *d_far[1:]), [(2 * rows, (len(d_far) - 1) * rows)]
    )
    far, far_gram, *dots = lax.optimization_barrier((far, far_gram, *dots))
    far = shared(far)
    (coeffs,) = call(functools.partial(coeffs_kernel, rows), "coeffs", dots, [(rows + 8, LANES)])
    grams = call(
        functools.partial(late_kernel, len(near), len(d_far), exchange),
        "late",
        (coeffs, qv_high, qv_low, near_gram, own_far, far_gram, *far),
        [(rows, LANES)] * cols if exchange else [(cols, rows, LANES)],
        [pltpu.VMEM((cols, rows, LANES), F32)],
    )
    scale = 1.0 / (length * nodes)
    (modes,) = call(modes_kernel, "modes", (coeffs, near[0]), [(rows, length)])
    if exchange:
        held = {0: coeffs}
        for bit in reversed(bits):
            for key in list(held):
                held[key ^ bit] = swapped(held[key] if key == 0 else held[key][0:8], "cols", bit)
        theirs = [held[key] for key in range(cols)]
        sums = [grams[0]] + [swapped(grams[i], "nodes", i) for i in reversed(range(1, nodes))]
        (tile,) = call(
            functools.partial(fifth_kernel, scale, nodes),
            "fifth",
            (*sums, *theirs),
            [(rows, rows)],
        )
    else:
        gram = grams[0]
        every = lax.all_gather(coeffs, "cols")
        mine = lax.axis_index("cols")
        parts = []
        for i in range(cols):
            block = lax.dynamic_index_in_dim(gram, mine ^ i, 0, keepdims=False)
            parts.append(
                every[i, 0:1, 0:rows] * block[:, 0:rows]
                + every[i, 1:2, 0:rows] * block[:, rows : 2 * rows]
            )
        partial = jnp.concatenate(parts, axis=1) * scale
        tile = lax.psum_scatter(partial, "nodes", scatter_dimension=1, tiled=True)
    return (modes, tile)


def solution(mesh):
    in_specs = (
        P("cols", ("groups", "nodes")),
        P(None, ("groups", "nodes")),
        P(("groups", "nodes")),
        P(("groups", "nodes"), None, None),
    )
    out_specs = (P("cols", ("groups", "nodes")), P(("groups", "cols"), "nodes"))
    return jax.shard_map(
        on_device, mesh=mesh, in_specs=in_specs, out_specs=out_specs, check_vma=False
    )
```
